128 devices in a mesh: dev: 128 (over y, x, z, core).
Axes of the slice: x: 4, y: 4, z: 4, core: 2. Of those that a mesh axis runs over, the one named last changes fastest.
Arguments:
- emb_a: float32 [131072, 128], P('dev'), may hold values from -6 to 6
- emb_b: float32 [131072, 128], P('dev'), may hold values from -6 to 6
- cat_a: int32 [131072], P('dev'), may hold values from 0 to 15
- cat_b: int32 [131072], P('dev'), may hold values from 0 to 15
- mass_a: float32 [131072], P('dev'), may hold values from 0.5 to 2
- mass_b: float32 [131072], P('dev'), may hold values from 0.5 to 2
- pair_list: int32 [128, 7], P('dev'), may hold values from 0 to 127, as said below
- pair_count: int32 [128], P('dev'), may hold values from 1 to 7, as said below
Outputs:
- mapped_a: float32 [131072, 128], P('dev')
- mapped_b: float32 [131072, 128], P('dev')
The draws below stay inside these ranges and needn't reach their ends.
Inputs may be any that keep to these rules, and one draw needn't show every extreme that they name: `pair_list`: row p lists, in rising order in its first pair_count[p] entries, distinct B slabs within 3 slabs of p, always including p itself; its other entries equal p. Some row lists all 7 slabs around it. pair_count[p] is the number of slabs listed in row p of pair_list; some row has 7.
All inputs are finite; a program needn't handle non-finite values.
Results may differ from the reference program's by a relative error of at most 0.0003.
Values sent between devices are 32-bit elements; how exact they have to be, the bound alone decides.
No kernel may reach another device: no remote copies, remote signals or barrier semaphores. Data moves between devices by JAX's collectives and lax.ppermute only.
A program may use at most 128 MiB of HBM per device.

```python
import math
import jax
import jax.numpy as jnp
from jax import lax

D = 128
SPAN = 3
SLOTS = 7
CATS = 16
ITERS = 2
NBLK = 128
NA = 131072
NB = 131072


def pair_layout(key):
    blocks = jnp.arange(NBLK, dtype=jnp.int32)
    offsets = jnp.arange(SLOTS, dtype=jnp.int32) - SPAN
    threshold = jax.random.randint(jax.random.fold_in(key, 11), (NBLK, 1), 1, SLOTS + 1)
    chosen = jax.random.randint(jax.random.fold_in(key, 12), (NBLK, SLOTS), 0, SLOTS)
    filled = jax.random.randint(jax.random.fold_in(key, 13), (), SPAN, NBLK - SPAN)
    active = chosen < threshold
    active = active | (blocks[:, None] == filled)
    active = active | (offsets[None, :] == 0)
    target = blocks[:, None] + offsets[None, :]
    active = active & (target >= 0) & (target < NBLK)
    ranks = jnp.where(active, offsets[None, :], offsets[None, :] + 4 * SLOTS)
    ranking = jnp.argsort(ranks, axis=1, stable=True)
    sorted_active = jnp.take_along_axis(active, ranking, axis=1)
    listed = jnp.where(sorted_active, jnp.take_along_axis(target, ranking, axis=1), blocks[:, None])
    counted = jnp.sum(active.astype(jnp.int32), axis=1)
    return (listed.astype(jnp.int32), counted.astype(jnp.int32))


def draw_pair_list(key, part):
    listed, counted = pair_layout(key)
    return listed


def draw_pair_count(key, part):
    listed, counted = pair_layout(key)
    return counted


def touch_ends(drawn, own_key, least, largest):
    dims = drawn.shape
    place = [jax.random.randint(jax.random.fold_in(own_key, axis), (), 0, dims[axis]) for axis in range(len(dims))]
    drawn = drawn.at[tuple(place)].set(least)
    longest = dims.index(max(dims))
    place[longest] = (place[longest] + 1) % dims[longest]
    return drawn.at[tuple(place)].set(largest)


def shard_levels(stream_key, shape, cuts, low, largest):
    def one(dim, blocks):
        heights = jax.random.uniform(jax.random.fold_in(jax.random.fold_in(stream_key, 6), dim), (blocks,), jnp.float32, low / len(cuts), largest / len(cuts))
        return jnp.repeat(jnp.exp(heights), shape[dim] // blocks).reshape((-1,) + (1,) * (len(shape) - dim - 1))

    level = one(*cuts[0])
    for cut in cuts[1:]:
        level = level * one(*cut)
    return level


def bell_draw(stream_key, shape, deviation, bound, split=(), held_as=jnp.bfloat16):
    array = jax.random.normal(stream_key, shape, jnp.float32) * deviation
    if len(split) > 0:
        array = shard_levels(stream_key, shape, split, -0.22, 0.18) * array
    return jnp.clip(array, min=-bound, max=bound).astype(held_as)


def setup_inputs(seed: int = 0) -> dict:
    key_of = jax.random.split(jax.random.key(seed), 9)
    return {
        "emb_a": bell_draw(key_of[0], (NA, D), 1.0, 6.0, ((0, 128),), jnp.float32),
        "emb_b": bell_draw(key_of[1], (NB, D), 1.0, 6.0, ((0, 128),), jnp.float32),
        "cat_a": touch_ends(jax.random.randint(key_of[2], (NA,), 0, CATS), jax.random.fold_in(key_of[2], 1), 0, CATS - 1).astype(jnp.int32),
        "cat_b": touch_ends(jax.random.randint(key_of[3], (NB,), 0, CATS), jax.random.fold_in(key_of[3], 1), 0, CATS - 1).astype(jnp.int32),
        "mass_a": jnp.clip(jnp.exp(math.log(2.0) - 1.3862944 * jax.random.uniform(key_of[4], (NA,), jnp.float32) ** shard_levels(key_of[4], (NA,), ((0, 128),), -0.2, 0.2)), 0.5, 2.0),
        "mass_b": jnp.clip(jnp.exp(math.log(2.0) - 1.3862944 * jax.random.uniform(key_of[5], (NB,), jnp.float32) ** shard_levels(key_of[5], (NB,), ((0, 128),), -0.2, 0.2)), 0.5, 2.0),
        "pair_list": draw_pair_list(jax.random.fold_in(key_of[8], 71), 0),
        "pair_count": draw_pair_count(jax.random.fold_in(key_of[8], 71), 0),
    }


penalty = 0.5
epsilon = 0.1
highest = lax.Precision.HIGHEST

def unit_rows(matrix):
    return matrix * lax.rsqrt(lax.optimization_barrier(jnp.sum(matrix * matrix, axis=1, keepdims=True)) + 1e-06)

def kernel_block(left_unit, left_cat, right_unit, right_cat):
    inner = lax.dot_general(left_unit, right_unit, (((1,), (1,)), ((), ())), precision=highest, preferred_element_type=jnp.float32)
    mismatch = (left_cat[:, None] != right_cat[None, :]).astype(jnp.float32)
    distance = 1.0 - inner + penalty * mismatch
    return jnp.exp(-distance / epsilon)

def reference(emb_a, emb_b, cat_a, cat_b, mass_a, mass_b, pair_list, pair_count):
    block_count = pair_list.shape[0]
    slab_rows = emb_a.shape[0] // block_count
    unit_a = unit_rows(emb_a).reshape(block_count, slab_rows, D)
    unit_b = unit_rows(emb_b).reshape(block_count, slab_rows, D)
    raw_a = emb_a.reshape(block_count, slab_rows, D)
    raw_b = emb_b.reshape(block_count, slab_rows, D)
    cats_a = cat_a.astype(jnp.float32).reshape(block_count, slab_rows)
    cats_b = cat_b.astype(jnp.float32).reshape(block_count, slab_rows)
    weight_a = mass_a.reshape(block_count, slab_rows)
    weight_b = mass_b.reshape(block_count, slab_rows)
    usable = (jnp.arange(SLOTS)[None, :] < pair_count[:, None]).astype(jnp.float32)
    blocks = jnp.arange(block_count, dtype=jnp.int32)

    def kernel_of(a_blk, slot):
        b_blk = pair_list[a_blk, slot]
        kernel = kernel_block(unit_a[a_blk], cats_a[a_blk], unit_b[b_blk], cats_b[b_blk]) * usable[a_blk, slot]
        return (b_blk, kernel)

    def row_sums(col_scale):

        def one_block(a_blk):
            summed = jnp.zeros((slab_rows,), jnp.float32)
            for slot in range(SLOTS):
                b_blk, kernel = kernel_of(a_blk, slot)
                summed = summed + jnp.dot(kernel, col_scale[b_blk], precision=highest, preferred_element_type=jnp.float32)
            return summed
        return lax.map(one_block, blocks)

    def col_sums(row_scale):

        def one_block(accum, a_blk):
            for slot in range(SLOTS):
                b_blk, kernel = kernel_of(a_blk, slot)
                accum = accum.at[b_blk].add(jnp.dot(row_scale[a_blk], kernel, precision=highest, preferred_element_type=jnp.float32))
            return (accum, None)
        accum, unused = lax.scan(one_block, jnp.zeros((block_count, slab_rows), jnp.float32), blocks)
        return accum
    col_scale = jnp.ones((block_count, slab_rows), jnp.float32)
    row_scale = jnp.ones((block_count, slab_rows), jnp.float32)
    for iteration in range(ITERS):
        row_scale = weight_a / row_sums(col_scale)
        col_scale = weight_b / col_sums(row_scale)

    def final_block(accum, a_blk):
        num_back, den_back = accum
        num_a = jnp.zeros((slab_rows, D), jnp.float32)
        den_a = jnp.zeros((slab_rows,), jnp.float32)
        scaled_a = row_scale[a_blk][:, None] * raw_a[a_blk]
        for slot in range(SLOTS):
            b_blk, kernel = kernel_of(a_blk, slot)
            column_part = col_scale[b_blk]
            num_a = num_a + jnp.dot(kernel, column_part[:, None] * raw_b[b_blk], precision=highest, preferred_element_type=jnp.float32)
            den_a = den_a + jnp.dot(kernel, column_part, precision=highest, preferred_element_type=jnp.float32)
            num_b = lax.dot_general(kernel, scaled_a, (((0,), (0,)), ((), ())), precision=highest, preferred_element_type=jnp.float32)
            den_b = jnp.dot(row_scale[a_blk], kernel, precision=highest, preferred_element_type=jnp.float32)
            num_back = num_back.at[b_blk].add(num_b)
            den_back = den_back.at[b_blk].add(den_b)
        return ((num_back, den_back), num_a / den_a[:, None])
    start = (jnp.zeros((block_count, slab_rows, D), jnp.float32), jnp.zeros((block_count, slab_rows), jnp.float32))
    (num_back, den_back), mapped_blocks = lax.scan(final_block, start, blocks)
    mapped_a = mapped_blocks.reshape(block_count * slab_rows, D)
    mapped_b = (num_back / den_back[:, :, None]).reshape(block_count * slab_rows, D)
    return (mapped_a, mapped_b)
```

```python
import math
from functools import partial

import jax
import jax.numpy as jnp
import ml_dtypes
import numpy as np
from jax import lax
from jax.experimental import pallas as pl
from jax.experimental.pallas import tpu as pltpu
from jax.sharding import PartitionSpec as P

ROWS = 1024
WIDTH = 128
SLAB = 136
CATS = 16
OFFSETS = (0, 1, 2, -2, -3, -1, 3)
SLOT = {offset: slot for slot, offset in enumerate(OFFSETS)}
SLOTS = 7
SCALE = 10.0 * math.log2(math.e)
F32 = jnp.float32
BF16 = jnp.bfloat16
VMEM = pl.BlockSpec(memory_space=pltpu.VMEM)
SMEM = pl.BlockSpec(memory_space=pltpu.SMEM)
MIB = 1024 * 1024


def three_parts(value):
    parts = []
    for _ in range(3):
        part = float(np.float32(value).astype(ml_dtypes.bfloat16))
        parts.append(part)
        value = value - part
    return parts


MATCH = three_parts(0.5 * SCALE)
BASE = three_parts(-1.5 * SCALE)


def held(array):
    return pltpu.with_memory_space_constraint(array, pltpu.VMEM)


def inside(shape, dtype=F32):
    return pltpu.VMEM(shape, dtype)


def plain(shape, dtype=F32):
    return jax.ShapeDtypeStruct(shape, dtype)


def local(body, outs, operands, scratch=(), limit=8, scalars=0, name=None):
    return pl.pallas_call(
        body,
        out_shape=outs,
        in_specs=[SMEM] * scalars + [VMEM] * (len(operands) - scalars),
        out_specs=tuple(VMEM for _ in outs) if isinstance(outs, tuple) else VMEM,
        scratch_shapes=list(scratch),
        compiler_params=pltpu.CompilerParams(vmem_limit_bytes=limit * MIB),
        name=name,
    )(*operands)


def routed(block, target):
    devices = lax.axis_size("dev")
    route = [(i, target(i)) for i in range(devices) if 0 <= target(i) < devices]
    return lax.ppermute(block, "dev", route)


def partner(block):
    return routed(block, lambda i: i + 1 - 2 * (i % 2))


def beside(block):
    return routed(block, lambda i: i - 1 + 2 * (i % 2))


def toward(block, chips):
    return routed(block, lambda i: i - 2 * chips * (1 - 2 * (i % 2)))


def away(block, chips):
    return routed(block, lambda i: i + 2 * chips * (1 - 2 * (i % 2)))


def halves(x):
    high = x.astype(BF16)
    return high, (x - high.astype(F32)).astype(BF16)


def lanes_summed(x):
    total = x[:, 0:WIDTH]
    for j in range(1, x.shape[1] // WIDTH):
        total = total + x[:, j * WIDTH : (j + 1) * WIDTH]
    return total


def slab_body(b_ref, cat_ref, mass_ref, slab_ref):
    slab_ref[0:WIDTH, :] = b_ref[...].T
    pad = jnp.zeros((SLAB - WIDTH - 2, ROWS), F32)
    slab_ref[WIDTH:SLAB, :] = jnp.concatenate([cat_ref[...].astype(F32), mass_ref[...], pad], axis=0)


def left_body(a_ref, cat_ref, mass_ref, left_ref, wide_mass_ref):
    a = a_ref[...]
    unit = a * lax.rsqrt(jnp.sum(a * a, axis=1, keepdims=True) + 1e-06) * SCALE
    high, low = halves(unit)
    lane = lax.broadcasted_iota(jnp.int32, (ROWS, WIDTH), 1)
    cat = jnp.broadcast_to(cat_ref[...].astype(F32), (WIDTH, ROWS)).T
    same = (lane % CATS).astype(F32) == cat
    match = jnp.where(lane < CATS, MATCH[0], jnp.where(lane < 2 * CATS, MATCH[1], MATCH[2]))
    base = jnp.where(lane == 3 * CATS, BASE[0], jnp.where(lane == 3 * CATS + 1, BASE[1], BASE[2]))
    bias = jnp.where(
        lane < 3 * CATS, jnp.where(same, match, 0.0), jnp.where(lane < 3 * CATS + 3, base, 0.0)
    )
    left_ref[:, 0:128] = high
    left_ref[:, 128:256] = low
    left_ref[:, 256:384] = high
    left_ref[:, 384:512] = bias.astype(BF16)
    wide_mass_ref[...] = jnp.broadcast_to(mass_ref[...], (WIDTH, ROWS)).T


def block_body(slot, on_ref, left_ref, slab_ref, kernel_ref, sum_ref, mass_ref, right):
    mass_ref[...] = slab_ref[WIDTH:SLAB, :]
    on = on_ref[slot]

    @pl.when(on > 0)
    def _():
        v = slab_ref[0:WIDTH, :]
        v = v * lax.rsqrt(jnp.sum(v * v, axis=0, keepdims=True) + 1e-06)
        high, low = halves(v)
        row = lax.broadcasted_iota(jnp.int32, (WIDTH, ROWS), 0)
        same = (row % CATS).astype(F32) == slab_ref[WIDTH : WIDTH + 1, :]
        bias = jnp.where(row < 3 * CATS, same.astype(F32), (row < 3 * CATS + 3).astype(F32))
        right[0:128, :] = high
        right[128:256, :] = high
        right[256:384, :] = low
        right[384:512, :] = bias.astype(BF16)
        step = 256
        for i in range(ROWS // step):
            rows = slice(i * step, (i + 1) * step)
            kernel = jnp.exp2(jnp.dot(left_ref[rows, :], right[...], preferred_element_type=F32))
            kernel_ref[rows, :] = kernel
            sum_ref[rows, :] = lanes_summed(kernel)

    @pl.when(on == 0)
    def _():
        kernel_ref[...] = jnp.zeros((ROWS, ROWS), F32)
        sum_ref[...] = jnp.zeros((ROWS, WIDTH), F32)


def column_parts(kernels, scale_ref, part_ref):
    step = 32
    part_ref[7:8, :] = jnp.zeros((1, ROWS), F32)
    for slot, offset in enumerate(OFFSETS):

        def add(i, total, slot=slot):
            rows = pl.ds(pl.multiple_of(i * step, step), step)
            scale = scale_ref[rows, :]
            product = kernels[slot][rows, :] * jnp.concatenate([scale] * 8, axis=1)
            for t in range(step // 8):
                total = total + product[t * 8 : (t + 1) * 8]
            return total

        total = lax.fori_loop(0, ROWS // step, add, jnp.zeros((8, ROWS), F32), unroll=2)
        part_ref[3 + offset : 4 + offset, :] = jnp.sum(total, axis=0, keepdims=True)


def first_body(*refs):
    kernels, sums, (mass_ref, part_ref, scale) = refs[:7], refs[7:14], refs[14:]
    total = sums[0][...]
    for more in sums[1:]:
        total = total + more[...]
    scale[...] = mass_ref[...] / jnp.sum(total, axis=1, keepdims=True)
    column_parts(kernels, scale, part_ref)


def mirrored(x):
    return jnp.concatenate([x[7 - m : 8 - m] for m in range(8)], axis=0)


def chip_body(part_ref, other_ref, out_ref):
    out_ref[...] = part_ref[...] + mirrored(other_ref[...])


def upper_body(one_ref, two_ref, three_ref, out_ref):
    zeros = jnp.zeros((2, ROWS), F32)
    out = jnp.concatenate([zeros, one_ref[0:6, :]], axis=0)
    out = out + jnp.concatenate([zeros, zeros, two_ref[0:4, :]], axis=0)
    out_ref[...] = out + jnp.concatenate([zeros, zeros, zeros, three_ref[0:2, :]], axis=0)


def column_scales(totals, masses):
    chip_ref, near_ref, far_ref = totals
    total = chip_ref[...] + near_ref[...] + mirrored(far_ref[...])
    scales = []
    for slot, offset in enumerate(OFFSETS):
        here = total[3 + offset : 4 + offset]
        known = here > 0.0
        scales.append(jnp.where(known, masses[slot][1:2, :] / jnp.where(known, here, 1.0), 0.0))
    return scales


def second_body(*refs):
    kernels, totals, masses = refs[:7], refs[7:10], refs[10:17]
    mass_ref, scale_ref, part_ref, columns = refs[17:]
    for slot, scale in enumerate(column_scales(totals, masses)):
        columns[slot : slot + 1, :] = scale
    step = 32

    def add(i, carry):
        rows = pl.ds(pl.multiple_of(i * step, step), step)
        total = jnp.zeros((step, WIDTH), F32)
        for slot in range(SLOTS):
            total = total + lanes_summed(kernels[slot][rows, :] * columns[slot : slot + 1, :])
        scale_ref[rows, :] = mass_ref[rows, :] / jnp.sum(total, axis=1, keepdims=True)
        return carry

    lax.fori_loop(0, ROWS // step, add, 0)
    column_parts(kernels, scale_ref, part_ref)


def scaled_body(scale_ref, a_ref, out_ref):
    high, low = halves((scale_ref[...] * a_ref[...]).T)
    out_ref[0:128, :] = high
    out_ref[128:256, :] = low


def back_body(scaled_ref, kernel_ref, *rest):
    terms, out_ref = rest[:-1], rest[-1]
    step = 256
    for j in range(ROWS // step):
        columns = slice(j * step, (j + 1) * step)
        high, low = halves(kernel_ref[:, columns])
        wide = jnp.dot(scaled_ref[...], high, preferred_element_type=F32)
        out = jnp.dot(scaled_ref[0:128, :], low, preferred_element_type=F32)
        out = out + wide[0:128] + wide[128:256]
        for term in terms:
            out = out + term[:, columns]
        out_ref[:, columns] = out


def back_map(scaled, kernel, *terms):
    operands = (held(scaled), held(kernel), *terms)
    return local(back_body, plain((WIDTH, ROWS)), operands, name="back_map")


def ahead_body(*refs):
    kernels, slabs, totals, masses = refs[:7], refs[7:14], refs[14:17], refs[17:24]
    out_ref, sums, weights, right = refs[24:]
    step = 256
    for slot, scale in enumerate(column_scales(totals, masses)):
        high, low = halves(slabs[slot][0:WIDTH, :] * scale)
        right[0:128, :] = high
        right[128:256, :] = low
        for i in range(ROWS // step):
            rows = slice(i * step, (i + 1) * step)
            kernel = kernels[slot][rows, :]
            weight = lanes_summed(kernel * scale)
            high, low = halves(kernel)
            across = (((1,), (1,)), ((), ()))
            wide = lax.dot_general(high, right[...], across, preferred_element_type=F32)
            part = lax.dot_general(low, right[0:128, :], across, preferred_element_type=F32)
            part = part + wide[:, 0:128] + wide[:, 128:256]
            if slot > 0:
                part = part + sums[rows, :]
                weight = weight + weights[rows, :]
            if slot < SLOTS - 1:
                sums[rows, :] = part
                weights[rows, :] = weight
            else:
                out_ref[rows, :] = part / jnp.sum(weight, axis=1, keepdims=True)


def last_body(*refs):
    own_ref, one_ref, two_ref, chip_ref, near_ref, far_ref, out_ref = refs
    total = chip_ref[3:4, :] + near_ref[3:4, :] + far_ref[4:5, :]
    out_ref[...] = ((own_ref[...] + one_ref[...] + two_ref[...]) / total).T


def exchanged(part):
    chip = local(chip_body, plain((8, ROWS)), (part, partner(part)), limit=4, name="chip_sum")
    one, two, three = toward(chip, 1), toward(chip, 2), toward(chip, 3)
    near = local(upper_body, plain((8, ROWS)), (one, two, three), limit=4, name="near_sum")
    return chip, near, partner(near)


def shards(emb_a, emb_b, cat_a, cat_b, mass_a, mass_b, pair_list, pair_count):
    position = lax.axis_index("dev")
    usable = jnp.arange(SLOTS) < pair_count[0]
    sign = 1 - 2 * (position % 2)
    targets = position + sign * jnp.array(OFFSETS, jnp.int32)
    listed = (pair_list[0][None, :] == targets[:, None]) & usable[None, :]
    on = jnp.any(listed, axis=1).astype(jnp.int32)

    slab = local(
        slab_body, plain((SLAB, ROWS)), (emb_b, cat_b[None], mass_b[None]), name="slab"
    )
    ahead_one = toward(slab, 1)
    other = partner(slab)
    behind_one = away(slab, 1)
    third = beside(ahead_one)
    slabs = (slab, other, ahead_one, behind_one, third, partner(ahead_one), partner(behind_one))

    left, wide_mass = local(
        left_body,
        (inside((ROWS, 4 * WIDTH), BF16), inside((ROWS, WIDTH))),
        (emb_a, cat_a[None], mass_a[None]),
        name="left",
    )
    kernels, sums, masses = [], [], []
    for slot in range(SLOTS):
        kernel, row_sum, mass = local(
            partial(block_body, slot),
            (inside((ROWS, ROWS)), inside((ROWS, WIDTH)), plain((8, ROWS))),
            (on, held(left), slabs[slot]),
            [pltpu.VMEM((4 * WIDTH, ROWS), BF16)],
            scalars=1,
            name="kernel_block",
        )
        kernels.append(kernel)
        sums.append(row_sum)
        masses.append(mass)

    held_kernels = [held(kernel) for kernel in kernels]
    part = local(
        first_body,
        plain((8, ROWS)),
        (*held_kernels, *[held(x) for x in sums], held(wide_mass)),
        [pltpu.VMEM((ROWS, WIDTH), F32)],
        name="first_scales",
    )
    totals = exchanged(part)
    row_scale, part = local(
        second_body,
        (inside((ROWS, WIDTH)), plain((8, ROWS))),
        (*held_kernels, *totals, *masses, held(wide_mass)),
        [pltpu.VMEM((8, ROWS), F32)],
        name="second_scales",
    )
    totals = exchanged(part)
    scaled = local(
        scaled_body, inside((2 * WIDTH, ROWS), BF16), (held(row_scale), emb_a), name="scaled_a"
    )
    third = beside(back_map(scaled, kernels[SLOT[-3]]))
    behind = partner(back_map(scaled, kernels[SLOT[3]]))
    ahead = partner(back_map(scaled, kernels[SLOT[-1]]))
    home = partner(back_map(scaled, kernels[SLOT[1]]))
    one = toward(back_map(scaled, kernels[SLOT[-2]], behind), 1)
    two = away(back_map(scaled, kernels[SLOT[2]], ahead, third), 1)
    own = back_map(scaled, kernels[SLOT[0]], home)
    mapped_a = local(
        ahead_body,
        plain((ROWS, WIDTH)),
        (*held_kernels, *slabs, *totals, *masses),
        [pltpu.VMEM((ROWS, WIDTH), F32)] * 2 + [pltpu.VMEM((2 * WIDTH, ROWS), BF16)],
        limit=12,
        name="ahead_map",
    )
    mapped_b = local(last_body, plain((ROWS, WIDTH)), (own, one, two, *totals), name="last")
    return (mapped_a, mapped_b)


def solution(mesh):
    placed = (
        P("dev", None),
        P("dev", None),
        P("dev"),
        P("dev"),
        P("dev"),
        P("dev"),
        P("dev", None),
        P("dev"),
    )
    return jax.shard_map(
        shards,
        mesh=mesh,
        in_specs=placed,
        out_specs=(P("dev", None), P("dev", None)),
        check_vma=False,
    )
```

```python
import math
from functools import partial

import jax
import jax.numpy as jnp
import ml_dtypes
import numpy as np
from jax import lax
from jax.experimental import pallas as pl
from jax.experimental.pallas import tpu as pltpu
from jax.sharding import PartitionSpec as P

ROWS = 1024
WIDTH = 128
SLAB = 136
CATS = 16
OFFSETS = (0, 1, 2, -2, -3, -1, 3)
SLOT = {offset: slot for slot, offset in enumerate(OFFSETS)}
SLOTS = 7
RELAYED = (2, 3)
SCALE = 10.0 * math.log2(math.e)
F32 = jnp.float32
BF16 = jnp.bfloat16
VMEM = pl.BlockSpec(memory_space=pltpu.VMEM)
SMEM = pl.BlockSpec(memory_space=pltpu.SMEM)
ANY = pl.BlockSpec(memory_space=pl.ANY)
MIB = 1024 * 1024


def three_parts(value):
    parts = []
    for _ in range(3):
        part = float(np.float32(value).astype(ml_dtypes.bfloat16))
        parts.append(part)
        value = value - part
    return parts


MATCH = three_parts(0.5 * SCALE)
BASE = three_parts(-1.5 * SCALE)


def held(array):
    return pltpu.with_memory_space_constraint(array, pltpu.VMEM)


def outside(array):
    return pltpu.with_memory_space_constraint(array, pltpu.HBM)


def inside(shape, dtype=F32):
    return pltpu.VMEM(shape, dtype)


def FLAGS(shape, dtype):
    return pltpu.SMEM(shape, dtype)


def flagged(array):
    return pltpu.with_memory_space_constraint(array, pltpu.SMEM)


def plain(shape, dtype=F32):
    return jax.ShapeDtypeStruct(shape, dtype)


def local(body, outs, operands, scratch=(), scalars=0, far=0, us=1, aliases=None, after=(), name=None):
    near = len(operands) - scalars - far
    used = len(operands)

    def with_tokens(*refs):
        body(*refs[:used], *refs[used + len(after) :])

    several = outs if isinstance(outs, tuple) else (outs,)
    spaces = [SMEM if getattr(out, "memory_space", None) is pltpu.SMEM else VMEM for out in several]
    return pl.pallas_call(
        with_tokens,
        out_shape=outs,
        in_specs=[SMEM] * scalars + [VMEM] * near + [ANY] * (far + len(after)),
        out_specs=tuple(spaces) if isinstance(outs, tuple) else spaces[0],
        scratch_shapes=list(scratch),
        input_output_aliases=aliases or {},
        compiler_params=pltpu.CompilerParams(vmem_limit_bytes=4 * MIB),
        cost_estimate=pl.CostEstimate(
            flops=int(us * 1e9), transcendentals=0, bytes_accessed=int(us * 3e6)
        ),
        name=name,
    )(*operands, *after)


def partner(block):
    devices = lax.axis_size("dev")
    return lax.ppermute(block, "dev", [(i, i + 1 - 2 * (i % 2)) for i in range(devices)])


def beside(block):
    devices = lax.axis_size("dev")
    route = [(i, (i - 1 + 2 * (i % 2)) % devices) for i in range(devices)]
    return lax.ppermute(block, "dev", route)


def relayed(block, chips, way):
    devices = lax.axis_size("dev")
    route = []
    for i in range(devices):
        target = i + 2 * chips * way * (1 - 2 * (i % 2))
        if target < 0:
            target = -1 - target
        if target >= devices:
            target = 2 * devices - 1 - target
        route.append((i, target))
    return lax.ppermute(block, "dev", route)


def toward(block, chips):
    return relayed(block, chips, -1)


def away(block, chips):
    return relayed(block, chips, 1)


def within(offset):
    position = lax.axis_index("dev")
    there = position + offset * (1 - 2 * (position % 2))
    return (there >= 0) & (there < lax.axis_size("dev"))


def halves(x):
    high = x.astype(BF16)
    return high, (x - high.astype(F32)).astype(BF16)


def lanes_summed(x):
    total = x[:, 0:WIDTH]
    for j in range(1, x.shape[1] // WIDTH):
        total = total + x[:, j * WIDTH : (j + 1) * WIDTH]
    return total


def fetch_all(copies, arrived):
    started = []
    for index, (source, target) in enumerate(copies):
        copy = pltpu.make_async_copy(source, target, arrived.at[index])
        copy.start()
        started.append(copy)
    for copy in started:
        copy.wait()


def slab_body(b_ref, cat_ref, mass_ref, slab_ref, b, cat, mass, arrived):
    fetch_all(((b_ref, b), (cat_ref, cat), (mass_ref, mass)), arrived)
    slab_ref[0:WIDTH, :] = b[...].T
    pad = jnp.zeros((SLAB - WIDTH - 2, ROWS), F32)
    slab_ref[WIDTH:SLAB, :] = jnp.concatenate([cat[...].astype(F32), mass[...], pad], axis=0)


def left_body(list_ref, count_ref, a_ref, cat_ref, mass_ref, *refs):
    left_ref, wide_mass_ref, on_ref, a, cat, mass, arrived = refs
    fetch_all(((a_ref, a), (cat_ref, cat), (mass_ref, mass)), arrived)
    position = lax.axis_index("dev")
    sign = 1 - 2 * (position % 2)
    for slot, offset in enumerate(OFFSETS):
        on = jnp.int32(0)
        for entry in range(SLOTS):
            here = (list_ref[0, entry] == position + sign * offset) & (entry < count_ref[0])
            on = jnp.where(here, jnp.int32(1), on)
        on_ref[slot] = on
    unit = a[...] * lax.rsqrt(jnp.sum(a[...] * a[...], axis=1, keepdims=True) + 1e-06) * SCALE
    high, low = halves(unit)
    lane = lax.broadcasted_iota(jnp.int32, (ROWS, WIDTH), 1)
    wide_cat = jnp.broadcast_to(cat[...].astype(F32), (WIDTH, ROWS)).T
    same = (lane % CATS).astype(F32) == wide_cat
    match = jnp.where(lane < CATS, MATCH[0], jnp.where(lane < 2 * CATS, MATCH[1], MATCH[2]))
    base = jnp.where(lane == 3 * CATS, BASE[0], jnp.where(lane == 3 * CATS + 1, BASE[1], BASE[2]))
    bias = jnp.where(
        lane < 3 * CATS, jnp.where(same, match, 0.0), jnp.where(lane < 3 * CATS + 3, base, 0.0)
    )
    left_ref[:, 0:128] = high
    left_ref[:, 128:256] = low
    left_ref[:, 256:384] = high
    left_ref[:, 384:512] = bias.astype(BF16)
    wide_mass_ref[...] = jnp.broadcast_to(mass[...], (WIDTH, ROWS)).T


def block_body(slot, on_ref, left_ref, slab_ref, *refs):
    kernel_ref, sum_ref, mass_ref = refs[-4 - (slot in RELAYED) :][:3]
    right = refs[-1]
    mass_ref[...] = slab_ref[WIDTH:SLAB, :]
    if slot in RELAYED:
        refs[-2][...] = slab_ref[...]

    @pl.when(on_ref[slot] > 0)
    def _():
        v = slab_ref[0:WIDTH, :]
        v = v * lax.rsqrt(jnp.sum(v * v, axis=0, keepdims=True) + 1e-06)
        high, low = halves(v)
        row = lax.broadcasted_iota(jnp.int32, (WIDTH, ROWS), 0)
        same = (row % CATS).astype(F32) == slab_ref[WIDTH : WIDTH + 1, :]
        bias = jnp.where(row < 3 * CATS, same.astype(F32), (row < 3 * CATS + 3).astype(F32))
        right[0:128, :] = high
        right[128:256, :] = high
        right[256:384, :] = low
        right[384:512, :] = bias.astype(BF16)
        step = 256
        for i in range(ROWS // step):
            rows = slice(i * step, (i + 1) * step)
            kernel = jnp.exp2(jnp.dot(left_ref[rows, :], right[...], preferred_element_type=F32))
            kernel_ref[slot, rows, :] = kernel
            total = lanes_summed(kernel)
            sum_ref[rows, :] = total if slot == 0 else sum_ref[rows, :] + total


def column_parts(on_ref, kernels, scale_ref, part_ref):
    step = 32
    part_ref[...] = jnp.zeros((8, ROWS), F32)
    for slot, offset in enumerate(OFFSETS):

        def add(i, total, slot=slot):
            rows = pl.ds(pl.multiple_of(i * step, step), step)
            scale = scale_ref[rows, :]
            product = kernels[slot, rows, :] * jnp.concatenate([scale] * 8, axis=1)
            for t in range(step // 8):
                total = total + product[t * 8 : (t + 1) * 8]
            return total

        @pl.when(on_ref[slot] > 0)
        def _(add=add, offset=offset):
            total = lax.fori_loop(0, ROWS // step, add, jnp.zeros((8, ROWS), F32), unroll=4)
            part_ref[3 + offset : 4 + offset, :] = jnp.sum(total, axis=0, keepdims=True)


def first_body(on_ref, kernels, sum_ref, mass_ref, kernels_out, part_ref, scale):
    scale[...] = mass_ref[...] / jnp.sum(sum_ref[...], axis=1, keepdims=True)
    column_parts(on_ref, kernels, scale, part_ref)


def mirrored(x):
    return jnp.concatenate([x[7 - m : 8 - m] for m in range(8)], axis=0)


def chip_body(part_ref, other_ref, out_ref):
    out_ref[...] = part_ref[...] + mirrored(other_ref[...])


def upper_body(one_ref, two_ref, three_ref, out_ref):
    out = jnp.zeros((8, ROWS), F32)
    for chips, ref in ((1, one_ref), (2, two_ref), (3, three_ref)):
        rows = jnp.where(within(2 * chips), ref[0 : 8 - 2 * chips, :], 0.0)
        out = out + jnp.concatenate([jnp.zeros((2 * chips, ROWS), F32), rows], axis=0)
    out_ref[...] = out


def column_scales(totals, masses):
    chip_ref, near_ref, far_ref = totals
    total = chip_ref[...] + near_ref[...] + mirrored(far_ref[...])
    scales = []
    for slot, offset in enumerate(OFFSETS):
        here = total[3 + offset : 4 + offset]
        known = here > 0.0
        scales.append(jnp.where(known, masses[slot][1:2, :] / jnp.where(known, here, 1.0), 0.0))
    return scales


def second_body(on_ref, kernels, *refs):
    totals, masses = refs[0:3], refs[3:10]
    mass_ref, kernels_out, scale_ref, part_ref = refs[10:]
    step = 32
    for slot, scale in enumerate(column_scales(totals, masses)):

        def add(i, carry, slot=slot, wide=jnp.broadcast_to(scale, (8, ROWS))):
            for t in range(0, step, 8):
                rows = pl.ds(pl.multiple_of(i * step + t, 8), 8)
                total = lanes_summed(kernels[slot, rows, :] * wide)
                scale_ref[rows, :] = total if slot == 0 else scale_ref[rows, :] + total
            return carry

        @pl.when(on_ref[slot] > 0)
        def _(add=add):
            lax.fori_loop(0, ROWS // step, add, 0, unroll=4)

    scale_ref[...] = mass_ref[...] / jnp.sum(scale_ref[...], axis=1, keepdims=True)
    column_parts(on_ref, kernels, scale_ref, part_ref)


def scaled_body(scale_ref, a_ref, out_ref):
    high, low = halves((scale_ref[...] * a_ref[...]).T)
    out_ref[0:128, :] = high
    out_ref[128:256, :] = low


def back_body(slot, on_ref, kernels, scaled_ref, *rest):
    terms, out_ref = rest[:-2], rest[-1]
    step = 256

    @pl.when(on_ref[slot] > 0)
    def _():
        for j in range(ROWS // step):
            columns = slice(j * step, (j + 1) * step)
            high, low = halves(kernels[slot, :, columns])
            wide = jnp.dot(scaled_ref[...], high, preferred_element_type=F32)
            out = jnp.dot(scaled_ref[0:128, :], low, preferred_element_type=F32)
            out = out + wide[0:128] + wide[128:256]
            for term in terms:
                out = out + term[:, columns]
            out_ref[:, columns] = out

    @pl.when(on_ref[slot] == 0)
    def _():
        out = jnp.zeros((WIDTH, ROWS), F32)
        for term in terms:
            out = out + term[...]
        out_ref[...] = out


def ahead_body(slot, last, on_ref, kernels, slab_ref, chip_ref, near_ref, far_ref, mass_ref, *refs):
    right = refs[-1]
    if last:
        sums, weights = refs[0:2]
        out_ref = refs[-2]
    else:
        sums, weights = refs[-3:-1]
    m = 3 + OFFSETS[slot]
    step = 256
    across = (((1,), (1,)), ((), ()))

    @pl.when(on_ref[slot] > 0)
    def _():
        total = chip_ref[m : m + 1, :] + near_ref[m : m + 1, :] + far_ref[7 - m : 8 - m, :]
        scale = mass_ref[1:2, :] / total
        high, low = halves(slab_ref[0:WIDTH, :] * scale)
        right[0:128, :] = high
        right[128:256, :] = low
        for i in range(ROWS // step):
            rows = slice(i * step, (i + 1) * step)
            kernel = kernels[slot, rows, :]
            weight = lanes_summed(kernel * scale)
            high, low = halves(kernel)
            wide = lax.dot_general(high, right[...], across, preferred_element_type=F32)
            part = lax.dot_general(low, right[0:128, :], across, preferred_element_type=F32)
            part = part + wide[:, 0:128] + wide[:, 128:256]
            sums[rows, :] = part if slot == 0 else part + sums[rows, :]
            weights[rows, :] = weight if slot == 0 else weight + weights[rows, :]

    if last:
        out_ref[...] = sums[...] / jnp.sum(weights[...], axis=1, keepdims=True)


def last_body(*refs):
    own_ref, one_ref, two_ref, chip_ref, near_ref, far_ref, out_ref = refs
    total = chip_ref[3:4, :] + near_ref[3:4, :] + far_ref[4:5, :]
    one = jnp.where(within(2), one_ref[...], 0.0)
    two = jnp.where(within(-2), two_ref[...], 0.0)
    out_ref[...] = ((own_ref[...] + one + two) / total).T


def exchanged(part):
    other = partner(part)
    chip = local(chip_body, plain((8, ROWS)), (part, other), name="chip_sum")
    one, two, three = toward(chip, 1), toward(chip, 2), toward(chip, 3)
    near = local(upper_body, plain((8, ROWS)), (one, two, three), name="near_sum")
    return (chip, near, partner(near)), (chip, three)


def shards(emb_a, emb_b, cat_a, cat_b, mass_a, mass_b, pair_list, pair_count):
    staged = [
        pltpu.VMEM((ROWS, WIDTH), F32),
        pltpu.VMEM((1, ROWS), jnp.int32),
        pltpu.VMEM((1, ROWS), F32),
        pltpu.SemaphoreType.DMA((3,)),
    ]
    slab = local(
        slab_body,
        plain((SLAB, ROWS)),
        tuple(map(outside, (emb_b, cat_b[None], mass_b[None]))),
        staged,
        far=3,
        name="slab",
    )
    ahead_one = toward(slab, 1)
    behind_one = away(slab, 1)
    other = partner(slab)
    left, wide_mass, on = local(
        left_body,
        (inside((ROWS, 4 * WIDTH), BF16), inside((ROWS, WIDTH)), FLAGS((8,), jnp.int32)),
        (pair_list, pair_count, *map(outside, (emb_a, cat_a[None], mass_a[None]))),
        staged,
        scalars=2,
        far=3,
        after=(slab,),
        name="left",
    )
    on = flagged(on)

    state, masses = (), [None] * SLOTS
    shapes = (inside((SLOTS, ROWS, ROWS)), inside((ROWS, WIDTH)), plain((8, ROWS)))

    def kernel_block(slot, slab):
        nonlocal state
        outs = shapes + ((plain((SLAB, ROWS)),) if slot in RELAYED else ())
        *state, masses[slot] = local(
            partial(block_body, slot),
            outs,
            (on, held(left), slab, *map(held, state)),
            [pltpu.VMEM((4 * WIDTH, ROWS), BF16)],
            scalars=1,
            us=2,
            aliases={3: 0, 4: 1} if state else None,
            name="kernel_block",
        )
        relayed = masses[slot]
        if slot in RELAYED:
            masses[slot] = state.pop()
        return relayed

    kernel_block(0, slab)
    kernel_block(1, other)
    shared_two = partner(kernel_block(3, behind_one))
    relayed = kernel_block(2, ahead_one)
    third = beside(relayed)
    shared = partner(relayed)
    kernel_block(6, shared_two)
    kernel_block(5, shared)
    kernel_block(4, third)
    slabs = (slab, other, ahead_one, behind_one, third, shared, shared_two)
    kernels, sums = state
    kernels, part = local(
        first_body,
        (shapes[0], plain((8, ROWS))),
        (on, held(kernels), held(sums), held(wide_mass)),
        [pltpu.VMEM((ROWS, WIDTH), F32)],
        scalars=1,
        us=3,
        aliases={1: 0},
        name="first_scales",
    )
    totals, _ = exchanged(part)
    kernels, row_scale, part = local(
        second_body,
        (shapes[0], inside((ROWS, WIDTH)), plain((8, ROWS))),
        (on, held(kernels), *totals, *masses, held(wide_mass)),
        scalars=1,
        us=5,
        aliases={1: 0},
        name="second_scales",
    )
    totals, steps = exchanged(part)
    scaled = local(
        scaled_body,
        inside((2 * WIDTH, ROWS), BF16),
        (held(row_scale), emb_a),
        after=steps[:1],
        name="scaled_a",
    )

    def back_map(offset, *terms, after=()):
        nonlocal kernels
        kernels, out = local(
            partial(back_body, SLOT[offset]),
            (shapes[0], plain((WIDTH, ROWS))),
            (on, held(kernels), held(scaled), *terms),
            scalars=1,
            us=2,
            aliases={1: 0},
            after=after,
            name="back_map",
        )
        return out

    third = beside(back_map(-3))
    behind = partner(back_map(3, after=totals[1:2]))
    ahead = partner(back_map(-1, after=totals[2:3]))
    home = partner(back_map(1))
    one = toward(back_map(-2, behind), 1)
    two = away(back_map(2, ahead, third), 1)
    state = ()
    for slot in range(SLOTS):
        last = slot == SLOTS - 1
        kernels, *state = local(
            partial(ahead_body, slot, last),
            (shapes[0], plain((ROWS, WIDTH))) if last else (shapes[0], shapes[1], shapes[1]),
            (on, held(kernels), slabs[slot], *totals, masses[slot], *map(held, state)),
            [pltpu.VMEM((2 * WIDTH, ROWS), BF16)],
            scalars=1,
            us=2,
            aliases={1: 0, 7: 1, 8: 2} if state and not last else {1: 0},
            name="ahead_map",
        )
    mapped_a = state[0]
    own = back_map(0, home)
    mapped_b = local(last_body, plain((ROWS, WIDTH)), (own, one, two, *totals), name="last")
    return (mapped_a, mapped_b)


def solution(mesh):
    placed = (
        P("dev", None),
        P("dev", None),
        P("dev"),
        P("dev"),
        P("dev"),
        P("dev"),
        P("dev", None),
        P("dev"),
    )
    return jax.shard_map(
        shards,
        mesh=mesh,
        in_specs=placed,
        out_specs=(P("dev", None), P("dev", None)),
        check_vma=False,
    )
```

```python
import math
from functools import partial

import jax
import jax.numpy as jnp
import ml_dtypes
import numpy as np
from jax import lax
from jax.experimental import pallas as pl
from jax.experimental.pallas import tpu as pltpu
from jax.sharding import PartitionSpec as P

ROWS = 1024
WIDTH = 128
SLAB = 136
CATS = 16
OFFSETS = (0, 1, 2, -2, -3, -1, 3)
SLOT = {offset: slot for slot, offset in enumerate(OFFSETS)}
SLOTS = 7
RELAYED = ()
SCALE = 10.0 * math.log2(math.e)
F32 = jnp.float32
BF16 = jnp.bfloat16
VMEM = pl.BlockSpec(memory_space=pltpu.VMEM)
SMEM = pl.BlockSpec(memory_space=pltpu.SMEM)
ANY = pl.BlockSpec(memory_space=pl.ANY)
MIB = 1024 * 1024


def three_parts(value):
    parts = []
    for _ in range(3):
        part = float(np.float32(value).astype(ml_dtypes.bfloat16))
        parts.append(part)
        value = value - part
    return parts


MATCH = three_parts(0.5 * SCALE)
BASE = three_parts(-1.5 * SCALE)


def held(array):
    return pltpu.with_memory_space_constraint(array, pltpu.VMEM)


def outside(array):
    return pltpu.with_memory_space_constraint(array, pltpu.HBM)


def inside(shape, dtype=F32):
    return pltpu.VMEM(shape, dtype)


def FLAGS(shape, dtype):
    return pltpu.SMEM(shape, dtype)


def flagged(array):
    return pltpu.with_memory_space_constraint(array, pltpu.SMEM)


def plain(shape, dtype=F32):
    return jax.ShapeDtypeStruct(shape, dtype)


def local(body, outs, operands, scratch=(), scalars=0, far=0, us=1, aliases=None, after=(), name=None):
    near = len(operands) - scalars - far
    used = len(operands)

    def with_tokens(*refs):
        body(*refs[:used], *refs[used + len(after) :])

    several = outs if isinstance(outs, tuple) else (outs,)
    spaces = [SMEM if getattr(out, "memory_space", None) is pltpu.SMEM else VMEM for out in several]
    return pl.pallas_call(
        with_tokens,
        out_shape=outs,
        in_specs=[SMEM] * scalars + [VMEM] * near + [ANY] * (far + len(after)),
        out_specs=tuple(spaces) if isinstance(outs, tuple) else spaces[0],
        scratch_shapes=list(scratch),
        input_output_aliases=aliases or {},
        compiler_params=pltpu.CompilerParams(vmem_limit_bytes=4 * MIB),
        cost_estimate=pl.CostEstimate(
            flops=int(us * 1e9), transcendentals=0, bytes_accessed=int(us * 3e6)
        ),
        name=name,
    )(*operands, *after)


def partner(block):
    devices = lax.axis_size("dev")
    return lax.ppermute(block, "dev", [(i, i + 1 - 2 * (i % 2)) for i in range(devices)])


def beside(block):
    devices = lax.axis_size("dev")
    route = [(i, (i - 1 + 2 * (i % 2)) % devices) for i in range(devices)]
    return lax.ppermute(block, "dev", route)


def relayed(block, chips, way):
    devices = lax.axis_size("dev")
    route = []
    for i in range(devices):
        target = i + 2 * chips * way * (1 - 2 * (i % 2))
        if target < 0:
            target = -1 - target
        if target >= devices:
            target = 2 * devices - 1 - target
        route.append((i, target))
    return lax.ppermute(block, "dev", route)


def toward(block, chips):
    return relayed(block, chips, -1)


def away(block, chips):
    return relayed(block, chips, 1)


def within(offset):
    position = lax.axis_index("dev")
    there = position + offset * (1 - 2 * (position % 2))
    return (there >= 0) & (there < lax.axis_size("dev"))


def halves(x):
    high = x.astype(BF16)
    return high, (x - high.astype(F32)).astype(BF16)


def lanes_summed(x):
    total = x[:, 0:WIDTH]
    for j in range(1, x.shape[1] // WIDTH):
        total = total + x[:, j * WIDTH : (j + 1) * WIDTH]
    return total


def fetch_all(copies, arrived):
    started = []
    for index, (source, target) in enumerate(copies):
        copy = pltpu.make_async_copy(source, target, arrived.at[index])
        copy.start()
        started.append(copy)
    for copy in started:
        copy.wait()


def slab_body(b_ref, cat_ref, mass_ref, slab_ref, b, cat, mass, arrived):
    fetch_all(((b_ref, b), (cat_ref, cat), (mass_ref, mass)), arrived)
    slab_ref[0:WIDTH, :] = b[...].T
    pad = jnp.zeros((SLAB - WIDTH - 2, ROWS), F32)
    slab_ref[WIDTH:SLAB, :] = jnp.concatenate([cat[...].astype(F32), mass[...], pad], axis=0)


def left_body(list_ref, count_ref, a_ref, cat_ref, mass_ref, *refs):
    left_ref, wide_mass_ref, on_ref, a, cat, mass, arrived = refs
    fetch_all(((a_ref, a), (cat_ref, cat), (mass_ref, mass)), arrived)
    position = lax.axis_index("dev")
    sign = 1 - 2 * (position % 2)
    for slot, offset in enumerate(OFFSETS):
        on = jnp.int32(0)
        for entry in range(SLOTS):
            here = (list_ref[0, entry] == position + sign * offset) & (entry < count_ref[0])
            on = jnp.where(here, jnp.int32(1), on)
        on_ref[slot] = on
    unit = a[...] * lax.rsqrt(jnp.sum(a[...] * a[...], axis=1, keepdims=True) + 1e-06) * SCALE
    high, low = halves(unit)
    lane = lax.broadcasted_iota(jnp.int32, (ROWS, WIDTH), 1)
    wide_cat = jnp.broadcast_to(cat[...].astype(F32), (WIDTH, ROWS)).T
    same = (lane % CATS).astype(F32) == wide_cat
    match = jnp.where(lane < CATS, MATCH[0], jnp.where(lane < 2 * CATS, MATCH[1], MATCH[2]))
    base = jnp.where(lane == 3 * CATS, BASE[0], jnp.where(lane == 3 * CATS + 1, BASE[1], BASE[2]))
    bias = jnp.where(
        lane < 3 * CATS, jnp.where(same, match, 0.0), jnp.where(lane < 3 * CATS + 3, base, 0.0)
    )
    left_ref[:, 0:128] = high
    left_ref[:, 128:256] = low
    left_ref[:, 256:384] = high
    left_ref[:, 384:512] = bias.astype(BF16)
    wide_mass_ref[...] = jnp.broadcast_to(mass[...], (WIDTH, ROWS)).T


def block_body(slot, on_ref, left_ref, slab_ref, *refs):
    kernel_ref, sum_ref, mass_ref = refs[-4 - (slot in RELAYED) :][:3]
    right = refs[-1]
    mass_ref[...] = slab_ref[WIDTH:SLAB, :]
    if slot in RELAYED:
        refs[-2][...] = slab_ref[...]

    @pl.when(on_ref[slot] > 0)
    def _():
        v = slab_ref[0:WIDTH, :]
        v = v * lax.rsqrt(jnp.sum(v * v, axis=0, keepdims=True) + 1e-06)
        high, low = halves(v)
        row = lax.broadcasted_iota(jnp.int32, (WIDTH, ROWS), 0)
        same = (row % CATS).astype(F32) == slab_ref[WIDTH : WIDTH + 1, :]
        bias = jnp.where(row < 3 * CATS, same.astype(F32), (row < 3 * CATS + 3).astype(F32))
        right[0:128, :] = high
        right[128:256, :] = high
        right[256:384, :] = low
        right[384:512, :] = bias.astype(BF16)
        step = 256
        for i in range(ROWS // step):
            rows = slice(i * step, (i + 1) * step)
            kernel = jnp.exp2(jnp.dot(left_ref[rows, :], right[...], preferred_element_type=F32))
            kernel_ref[slot, rows, :] = kernel
            total = lanes_summed(kernel)
            sum_ref[rows, :] = total if slot == 0 else sum_ref[rows, :] + total


def column_parts(on_ref, kernels, scale_ref, part_ref):
    step = 32
    part_ref[...] = jnp.zeros((8, ROWS), F32)
    for slot, offset in enumerate(OFFSETS):

        def add(i, total, slot=slot):
            rows = pl.ds(pl.multiple_of(i * step, step), step)
            scale = scale_ref[rows, :]
            product = kernels[slot, rows, :] * jnp.concatenate([scale] * 8, axis=1)
            for t in range(step // 8):
                total = total + product[t * 8 : (t + 1) * 8]
            return total

        @pl.when(on_ref[slot] > 0)
        def _(add=add, offset=offset):
            total = lax.fori_loop(0, ROWS // step, add, jnp.zeros((8, ROWS), F32), unroll=4)
            part_ref[3 + offset : 4 + offset, :] = jnp.sum(total, axis=0, keepdims=True)


def first_body(on_ref, kernels, sum_ref, mass_ref, kernels_out, part_ref, scale):
    scale[...] = mass_ref[...] / jnp.sum(sum_ref[...], axis=1, keepdims=True)
    column_parts(on_ref, kernels, scale, part_ref)


def mirrored(x):
    return jnp.concatenate([x[7 - m : 8 - m] for m in range(8)], axis=0)


def chip_body(part_ref, other_ref, out_ref):
    out_ref[...] = part_ref[...] + mirrored(other_ref[...])


def upper_body(one_ref, two_ref, three_ref, out_ref):
    out = jnp.zeros((8, ROWS), F32)
    for chips, ref in ((1, one_ref), (2, two_ref), (3, three_ref)):
        rows = jnp.where(within(2 * chips), ref[0 : 8 - 2 * chips, :], 0.0)
        out = out + jnp.concatenate([jnp.zeros((2 * chips, ROWS), F32), rows], axis=0)
    out_ref[...] = out


def column_scales(totals, masses):
    chip_ref, near_ref, far_ref = totals
    total = chip_ref[...] + near_ref[...] + mirrored(far_ref[...])
    scales = []
    for slot, offset in enumerate(OFFSETS):
        here = total[3 + offset : 4 + offset]
        known = here > 0.0
        scales.append(jnp.where(known, masses[slot][1:2, :] / jnp.where(known, here, 1.0), 0.0))
    return scales


def second_body(on_ref, kernels, *refs):
    totals, masses = refs[0:3], refs[3:10]
    mass_ref, kernels_out, scale_ref, part_ref = refs[10:]
    step = 32
    for slot, scale in enumerate(column_scales(totals, masses)):

        def add(i, carry, slot=slot, wide=jnp.broadcast_to(scale, (8, ROWS))):
            for t in range(0, step, 8):
                rows = pl.ds(pl.multiple_of(i * step + t, 8), 8)
                total = lanes_summed(kernels[slot, rows, :] * wide)
                scale_ref[rows, :] = total if slot == 0 else scale_ref[rows, :] + total
            return carry

        @pl.when(on_ref[slot] > 0)
        def _(add=add):
            lax.fori_loop(0, ROWS // step, add, 0, unroll=4)

    scale_ref[...] = mass_ref[...] / jnp.sum(scale_ref[...], axis=1, keepdims=True)
    column_parts(on_ref, kernels, scale_ref, part_ref)


def scaled_body(scale_ref, a_ref, out_ref):
    high, low = halves((scale_ref[...] * a_ref[...]).T)
    out_ref[0:128, :] = high
    out_ref[128:256, :] = low


def back_body(slot, on_ref, kernels, scaled_ref, *rest):
    terms, out_ref = rest[:-2], rest[-1]
    step = 256

    @pl.when(on_ref[slot] > 0)
    def _():
        for j in range(ROWS // step):
            columns = slice(j * step, (j + 1) * step)
            high, low = halves(kernels[slot, :, columns])
            wide = jnp.dot(scaled_ref[...], high, preferred_element_type=F32)
            out = jnp.dot(scaled_ref[0:128, :], low, preferred_element_type=F32)
            out = out + wide[0:128] + wide[128:256]
            for term in terms:
                out = out + term[:, columns]
            out_ref[:, columns] = out

    @pl.when(on_ref[slot] == 0)
    def _():
        out = jnp.zeros((WIDTH, ROWS), F32)
        for term in terms:
            out = out + term[...]
        out_ref[...] = out


def ahead_body(slot, last, on_ref, kernels, slab_ref, chip_ref, near_ref, far_ref, mass_ref, *refs):
    right = refs[-1]
    if last:
        sums, weights = refs[0:2]
        out_ref = refs[-2]
    else:
        sums, weights = refs[-3:-1]
    m = 3 + OFFSETS[slot]
    step = 256
    across = (((1,), (1,)), ((), ()))

    @pl.when(on_ref[slot] > 0)
    def _():
        total = chip_ref[m : m + 1, :] + near_ref[m : m + 1, :] + far_ref[7 - m : 8 - m, :]
        scale = mass_ref[1:2, :] / total
        high, low = halves(slab_ref[0:WIDTH, :] * scale)
        right[0:128, :] = high
        right[128:256, :] = low
        for i in range(ROWS // step):
            rows = slice(i * step, (i + 1) * step)
            kernel = kernels[slot, rows, :]
            weight = lanes_summed(kernel * scale)
            high, low = halves(kernel)
            wide = lax.dot_general(high, right[...], across, preferred_element_type=F32)
            part = lax.dot_general(low, right[0:128, :], across, preferred_element_type=F32)
            part = part + wide[:, 0:128] + wide[:, 128:256]
            sums[rows, :] = part if slot == 0 else part + sums[rows, :]
            weights[rows, :] = weight if slot == 0 else weight + weights[rows, :]

    if last:
        out_ref[...] = sums[...] / jnp.sum(weights[...], axis=1, keepdims=True)


def last_body(*refs):
    own_ref, one_ref, two_ref, chip_ref, near_ref, far_ref, out_ref = refs
    total = chip_ref[3:4, :] + near_ref[3:4, :] + far_ref[4:5, :]
    one = jnp.where(within(2), one_ref[...], 0.0)
    two = jnp.where(within(-2), two_ref[...], 0.0)
    out_ref[...] = ((own_ref[...] + one + two) / total).T


def exchanged(part):
    other = partner(part)
    chip = local(chip_body, plain((8, ROWS)), (part, other), name="chip_sum")
    one, two, three = toward(chip, 1), toward(chip, 2), toward(chip, 3)
    near = local(upper_body, plain((8, ROWS)), (one, two, three), name="near_sum")
    return (chip, near, partner(near)), (chip, three)


def shards(emb_a, emb_b, cat_a, cat_b, mass_a, mass_b, pair_list, pair_count):
    staged = [
        pltpu.VMEM((ROWS, WIDTH), F32),
        pltpu.VMEM((1, ROWS), jnp.int32),
        pltpu.VMEM((1, ROWS), F32),
        pltpu.SemaphoreType.DMA((3,)),
    ]
    slab = local(
        slab_body,
        plain((SLAB, ROWS)),
        tuple(map(outside, (emb_b, cat_b[None], mass_b[None]))),
        staged,
        far=3,
        name="slab",
    )
    ahead_one = toward(slab, 1)
    behind_one = away(slab, 1)
    other = partner(slab)
    left, wide_mass, on = local(
        left_body,
        (inside((ROWS, 4 * WIDTH), BF16), inside((ROWS, WIDTH)), FLAGS((8,), jnp.int32)),
        (pair_list, pair_count, *map(outside, (emb_a, cat_a[None], mass_a[None]))),
        staged,
        scalars=2,
        far=3,
        after=(slab,),
        name="left",
    )
    on = flagged(on)

    state, masses = (), [None] * SLOTS
    shapes = (inside((SLOTS, ROWS, ROWS)), inside((ROWS, WIDTH)), plain((8, ROWS)))

    def kernel_block(slot, slab):
        nonlocal state
        outs = shapes + ((plain((SLAB, ROWS)),) if slot in RELAYED else ())
        *state, masses[slot] = local(
            partial(block_body, slot),
            outs,
            (on, held(left), slab, *map(held, state)),
            [pltpu.VMEM((4 * WIDTH, ROWS), BF16)],
            scalars=1,
            us=2,
            aliases={3: 0, 4: 1} if state else None,
            name="kernel_block",
        )
        relayed = masses[slot]
        if slot in RELAYED:
            masses[slot] = state.pop()
        return relayed

    kernel_block(0, slab)
    kernel_block(1, other)
    third = beside(ahead_one)
    shared_two = partner(behind_one)
    shared = partner(ahead_one)
    kernel_block(3, behind_one)
    kernel_block(2, ahead_one)
    kernel_block(6, shared_two)
    kernel_block(5, shared)
    kernel_block(4, third)
    slabs = (slab, other, ahead_one, behind_one, third, shared, shared_two)
    kernels, sums = state
    kernels, part = local(
        first_body,
        (shapes[0], plain((8, ROWS))),
        (on, held(kernels), held(sums), held(wide_mass)),
        [pltpu.VMEM((ROWS, WIDTH), F32)],
        scalars=1,
        us=3,
        aliases={1: 0},
        name="first_scales",
    )
    totals, _ = exchanged(part)
    kernels, row_scale, part = local(
        second_body,
        (shapes[0], inside((ROWS, WIDTH)), plain((8, ROWS))),
        (on, held(kernels), *totals, *masses, held(wide_mass)),
        scalars=1,
        us=5,
        aliases={1: 0},
        name="second_scales",
    )
    totals, steps = exchanged(part)
    scaled = local(
        scaled_body,
        inside((2 * WIDTH, ROWS), BF16),
        (held(row_scale), emb_a),
        after=steps[:1],
        name="scaled_a",
    )

    def back_map(offset, *terms, after=()):
        nonlocal kernels
        kernels, out = local(
            partial(back_body, SLOT[offset]),
            (shapes[0], plain((WIDTH, ROWS))),
            (on, held(kernels), held(scaled), *terms),
            scalars=1,
            us=2,
            aliases={1: 0},
            after=after,
            name="back_map",
        )
        return out

    third = beside(back_map(-3))
    behind = partner(back_map(3, after=totals[1:2]))
    ahead = partner(back_map(-1, after=totals[2:3]))
    home = partner(back_map(1))
    one = toward(back_map(-2, behind), 1)
    two = away(back_map(2, ahead, third), 1)
    state = ()
    for slot in range(SLOTS):
        last = slot == SLOTS - 1
        kernels, *state = local(
            partial(ahead_body, slot, last),
            (shapes[0], plain((ROWS, WIDTH))) if last else (shapes[0], shapes[1], shapes[1]),
            (on, held(kernels), slabs[slot], *totals, masses[slot], *map(held, state)),
            [pltpu.VMEM((2 * WIDTH, ROWS), BF16)],
            scalars=1,
            us=2,
            aliases={1: 0, 7: 1, 8: 2} if state and not last else {1: 0},
            name="ahead_map",
        )
    mapped_a = state[0]
    own = back_map(0, home)
    mapped_b = local(last_body, plain((ROWS, WIDTH)), (own, one, two, *totals), name="last")
    return (mapped_a, mapped_b)


def solution(mesh):
    placed = (
        P("dev", None),
        P("dev", None),
        P("dev"),
        P("dev"),
        P("dev"),
        P("dev"),
        P("dev", None),
        P("dev"),
    )
    return jax.shard_map(
        shards,
        mesh=mesh,
        in_specs=placed,
        out_specs=(P("dev", None), P("dev", None)),
        check_vma=False,
    )
```

```python
import math
from functools import partial

import jax
import jax.numpy as jnp
import ml_dtypes
import numpy as np
from jax import lax
from jax.experimental import pallas as pl
from jax.experimental.pallas import tpu as pltpu
from jax.sharding import PartitionSpec as P

ROWS = 1024
WIDTH = 128
SLAB = 136
CATS = 16
OFFSETS = (0, 1, 2, -2, -3, -1, 3)
SLOT = {offset: slot for slot, offset in enumerate(OFFSETS)}
SLOTS = 7
RELAYED = ()
SCALE = 10.0 * math.log2(math.e)
F32 = jnp.float32
BF16 = jnp.bfloat16
VMEM = pl.BlockSpec(memory_space=pltpu.VMEM)
SMEM = pl.BlockSpec(memory_space=pltpu.SMEM)
ANY = pl.BlockSpec(memory_space=pl.ANY)
MIB = 1024 * 1024


def three_parts(value):
    parts = []
    for _ in range(3):
        part = float(np.float32(value).astype(ml_dtypes.bfloat16))
        parts.append(part)
        value = value - part
    return parts


MATCH = three_parts(0.5 * SCALE)
BASE = three_parts(-1.5 * SCALE)


def held(array):
    return pltpu.with_memory_space_constraint(array, pltpu.VMEM)


def outside(array):
    return pltpu.with_memory_space_constraint(array, pltpu.HBM)


def inside(shape, dtype=F32):
    return pltpu.VMEM(shape, dtype)


def FLAGS(shape, dtype):
    return pltpu.SMEM(shape, dtype)


def flagged(array):
    return pltpu.with_memory_space_constraint(array, pltpu.SMEM)


def plain(shape, dtype=F32):
    return jax.ShapeDtypeStruct(shape, dtype)


def local(body, outs, operands, scratch=(), scalars=0, far=0, us=1, aliases=None, after=(), sent=(), name=None):
    near = len(operands) - scalars - far
    used = len(operands)

    def with_tokens(*refs):
        body(*refs[:used], *refs[used + len(after) :])

    several = outs if isinstance(outs, tuple) else (outs,)
    spaces = [SMEM if getattr(out, "memory_space", None) is pltpu.SMEM else VMEM for out in several]
    for index in sent:
        spaces[index] = ANY
    return pl.pallas_call(
        with_tokens,
        out_shape=outs,
        in_specs=[SMEM] * scalars + [VMEM] * near + [ANY] * (far + len(after)),
        out_specs=tuple(spaces) if isinstance(outs, tuple) else spaces[0],
        scratch_shapes=list(scratch),
        input_output_aliases=aliases or {},
        compiler_params=pltpu.CompilerParams(vmem_limit_bytes=4 * MIB),
        cost_estimate=pl.CostEstimate(
            flops=int(us * 1e9), transcendentals=0, bytes_accessed=int(us * 3e6)
        ),
        name=name,
    )(*operands, *after)


def partner(block):
    devices = lax.axis_size("dev")
    return lax.ppermute(block, "dev", [(i, i + 1 - 2 * (i % 2)) for i in range(devices)])


def beside(block):
    devices = lax.axis_size("dev")
    route = [(i, (i - 1 + 2 * (i % 2)) % devices) for i in range(devices)]
    return lax.ppermute(block, "dev", route)


def relayed(block, chips, way):
    devices = lax.axis_size("dev")
    route = []
    for i in range(devices):
        target = i + 2 * chips * way * (1 - 2 * (i % 2))
        if target < 0:
            target = -1 - target
        if target >= devices:
            target = 2 * devices - 1 - target
        route.append((i, target))
    return lax.ppermute(block, "dev", route)


def toward(block, chips):
    return relayed(block, chips, -1)


def away(block, chips):
    return relayed(block, chips, 1)


def within(offset):
    position = lax.axis_index("dev")
    there = position + offset * (1 - 2 * (position % 2))
    return (there >= 0) & (there < lax.axis_size("dev"))


def halves(x):
    high = x.astype(BF16)
    return high, (x - high.astype(F32)).astype(BF16)


def lanes_summed(x):
    total = x[:, 0:WIDTH]
    for j in range(1, x.shape[1] // WIDTH):
        total = total + x[:, j * WIDTH : (j + 1) * WIDTH]
    return total


def fetch_all(copies, arrived):
    started = []
    for index, (source, target) in enumerate(copies):
        copy = pltpu.make_async_copy(source, target, arrived.at[index])
        copy.start()
        started.append(copy)
    for copy in started:
        copy.wait()


def slab_body(b_ref, cat_ref, mass_ref, slab_ref, b, cat, mass, arrived):
    fetch_all(((b_ref, b), (cat_ref, cat), (mass_ref, mass)), arrived)
    slab_ref[0:WIDTH, :] = b[...].T
    pad = jnp.zeros((SLAB - WIDTH - 2, ROWS), F32)
    slab_ref[WIDTH:SLAB, :] = jnp.concatenate([cat[...].astype(F32), mass[...], pad], axis=0)


def left_body(list_ref, count_ref, a_ref, cat_ref, mass_ref, *refs):
    left_ref, wide_mass_ref, on_ref, a, cat, mass, arrived = refs
    fetch_all(((a_ref, a), (cat_ref, cat), (mass_ref, mass)), arrived)
    position = lax.axis_index("dev")
    sign = 1 - 2 * (position % 2)
    for slot, offset in enumerate(OFFSETS):
        on = jnp.int32(0)
        for entry in range(SLOTS):
            here = (list_ref[0, entry] == position + sign * offset) & (entry < count_ref[0])
            on = jnp.where(here, jnp.int32(1), on)
        on_ref[slot] = on
    unit = a[...] * lax.rsqrt(jnp.sum(a[...] * a[...], axis=1, keepdims=True) + 1e-06) * SCALE
    high, low = halves(unit)
    lane = lax.broadcasted_iota(jnp.int32, (ROWS, WIDTH), 1)
    wide_cat = jnp.broadcast_to(cat[...].astype(F32), (WIDTH, ROWS)).T
    same = (lane % CATS).astype(F32) == wide_cat
    match = jnp.where(lane < CATS, MATCH[0], jnp.where(lane < 2 * CATS, MATCH[1], MATCH[2]))
    base = jnp.where(lane == 3 * CATS, BASE[0], jnp.where(lane == 3 * CATS + 1, BASE[1], BASE[2]))
    bias = jnp.where(
        lane < 3 * CATS, jnp.where(same, match, 0.0), jnp.where(lane < 3 * CATS + 3, base, 0.0)
    )
    left_ref[:, 0:128] = high
    left_ref[:, 128:256] = low
    left_ref[:, 256:384] = high
    left_ref[:, 384:512] = bias.astype(BF16)
    wide_mass_ref[...] = jnp.broadcast_to(mass[...], (WIDTH, ROWS)).T


def block_body(slot, on_ref, left_ref, slab_ref, *refs):
    kernel_ref, sum_ref, mass_ref = refs[-4 - (slot in RELAYED) :][:3]
    right = refs[-1]
    mass_ref[...] = slab_ref[WIDTH:SLAB, :]
    if slot in RELAYED:
        refs[-2][...] = slab_ref[...]

    @pl.when(on_ref[slot] > 0)
    def _():
        v = slab_ref[0:WIDTH, :]
        v = v * lax.rsqrt(jnp.sum(v * v, axis=0, keepdims=True) + 1e-06)
        high, low = halves(v)
        row = lax.broadcasted_iota(jnp.int32, (WIDTH, ROWS), 0)
        same = (row % CATS).astype(F32) == slab_ref[WIDTH : WIDTH + 1, :]
        bias = jnp.where(row < 3 * CATS, same.astype(F32), (row < 3 * CATS + 3).astype(F32))
        right[0:128, :] = high
        right[128:256, :] = high
        right[256:384, :] = low
        right[384:512, :] = bias.astype(BF16)
        step = 256
        for i in range(ROWS // step):
            rows = slice(i * step, (i + 1) * step)
            kernel = jnp.exp2(jnp.dot(left_ref[rows, :], right[...], preferred_element_type=F32))
            kernel_ref[slot, rows, :] = kernel
            total = lanes_summed(kernel)
            sum_ref[rows, :] = total if slot == 0 else sum_ref[rows, :] + total


def column_parts(on_ref, kernels, scale_ref, part_ref):
    step = 32
    part_ref[...] = jnp.zeros((8, ROWS), F32)
    for slot, offset in enumerate(OFFSETS):

        def add(i, total, slot=slot):
            rows = pl.ds(pl.multiple_of(i * step, step), step)
            scale = scale_ref[rows, :]
            product = kernels[slot, rows, :] * jnp.concatenate([scale] * 8, axis=1)
            for t in range(step // 8):
                total = total + product[t * 8 : (t + 1) * 8]
            return total

        @pl.when(on_ref[slot] > 0)
        def _(add=add, offset=offset):
            total = lax.fori_loop(0, ROWS // step, add, jnp.zeros((8, ROWS), F32), unroll=8)
            part_ref[3 + offset : 4 + offset, :] = jnp.sum(total, axis=0, keepdims=True)


def first_body(on_ref, kernels, sum_ref, mass_ref, kernels_out, part_ref, scale):
    scale[...] = mass_ref[...] / jnp.sum(sum_ref[...], axis=1, keepdims=True)
    column_parts(on_ref, kernels, scale, part_ref)


def mirrored(x):
    return jnp.concatenate([x[7 - m : 8 - m] for m in range(8)], axis=0)


def chip_body(part_ref, other_ref, out_ref):
    out_ref[...] = part_ref[...] + mirrored(other_ref[...])


def upper_body(one_ref, two_ref, three_ref, out_ref):
    out = jnp.zeros((8, ROWS), F32)
    for chips, ref in ((1, one_ref), (2, two_ref), (3, three_ref)):
        rows = jnp.where(within(2 * chips), ref[0 : 8 - 2 * chips, :], 0.0)
        out = out + jnp.concatenate([jnp.zeros((2 * chips, ROWS), F32), rows], axis=0)
    out_ref[...] = out


def column_scales(totals, masses):
    chip_ref, near_ref, far_ref = totals
    total = chip_ref[...] + near_ref[...] + mirrored(far_ref[...])
    scales = []
    for slot, offset in enumerate(OFFSETS):
        here = total[3 + offset : 4 + offset]
        known = here > 0.0
        scales.append(jnp.where(known, masses[slot][1:2, :] / jnp.where(known, here, 1.0), 0.0))
    return scales


def second_body(on_ref, kernels, *refs):
    totals, masses = refs[0:3], refs[3:10]
    mass_ref, kernels_out, scale_ref, part_ref = refs[10:]
    step = 32
    for slot, scale in enumerate(column_scales(totals, masses)):

        def add(i, carry, slot=slot, wide=jnp.broadcast_to(scale, (8, ROWS))):
            for t in range(0, step, 8):
                rows = pl.ds(pl.multiple_of(i * step + t, 8), 8)
                total = lanes_summed(kernels[slot, rows, :] * wide)
                scale_ref[rows, :] = total if slot == 0 else scale_ref[rows, :] + total
            return carry

        @pl.when(on_ref[slot] > 0)
        def _(add=add):
            lax.fori_loop(0, ROWS // step, add, 0, unroll=8)

    scale_ref[...] = mass_ref[...] / jnp.sum(scale_ref[...], axis=1, keepdims=True)
    column_parts(on_ref, kernels, scale_ref, part_ref)


def scaled_body(scale_ref, a_ref, out_ref):
    high, low = halves((scale_ref[...] * a_ref[...]).T)
    out_ref[0:128, :] = high
    out_ref[128:256, :] = low


def back_body(slot, on_ref, kernels, scaled_ref, *rest):
    terms, out_ref = rest[:-2], rest[-1]
    step = 256

    @pl.when(on_ref[slot] > 0)
    def _():
        for j in range(ROWS // step):
            columns = slice(j * step, (j + 1) * step)
            high, low = halves(kernels[slot, :, columns])
            wide = jnp.dot(scaled_ref[...], high, preferred_element_type=F32)
            out = jnp.dot(scaled_ref[0:128, :], low, preferred_element_type=F32)
            out = out + wide[0:128] + wide[128:256]
            for term in terms:
                out = out + term[:, columns]
            out_ref[:, columns] = out

    @pl.when(on_ref[slot] == 0)
    def _():
        out = jnp.zeros((WIDTH, ROWS), F32)
        for term in terms:
            out = out + term[...]
        out_ref[...] = out


def ahead_body(slot, on_ref, kernels, slab_ref, chip_ref, near_ref, far_ref, mass_ref, *refs):
    final = slot == SLOTS - 1
    if final:
        sums, weights, kernels_out, out_ref, right, staged, sent = refs
    else:
        sums, weights, right = refs[-3:]
    m = 3 + OFFSETS[slot]
    step = 256
    across = (((1,), (1,)), ((), ()))
    chunks = [slice(i * step, (i + 1) * step) for i in range(ROWS // step)]

    def send(i):
        return pltpu.make_async_copy(staged.at[chunks[i], :], out_ref.at[chunks[i], :], sent.at[i])

    @pl.when(on_ref[slot] > 0)
    def _():
        total = chip_ref[m : m + 1, :] + near_ref[m : m + 1, :] + far_ref[7 - m : 8 - m, :]
        scale = mass_ref[1:2, :] / total
        high, low = halves(slab_ref[0:WIDTH, :] * scale)
        right[0:128, :] = high
        right[128:256, :] = low
        for i, rows in enumerate(chunks):
            kernel = kernels[slot, rows, :]
            weight = lanes_summed(kernel * scale)
            high, low = halves(kernel)
            wide = lax.dot_general(high, right[...], across, preferred_element_type=F32)
            part = lax.dot_general(low, right[0:128, :], across, preferred_element_type=F32)
            part = part + wide[:, 0:128] + wide[:, 128:256]
            if slot > 0:
                part = part + sums[rows, :]
                weight = weight + weights[rows, :]
            if final:
                staged[rows, :] = part / jnp.sum(weight, axis=1, keepdims=True)
                send(i).start()
            else:
                sums[rows, :] = part
                weights[rows, :] = weight

    if final:

        @pl.when(on_ref[slot] == 0)
        def _():
            for i, rows in enumerate(chunks):
                staged[rows, :] = sums[rows, :] / jnp.sum(weights[rows, :], axis=1, keepdims=True)
                send(i).start()

        for i in range(len(chunks)):
            send(i).wait()


def last_body(own_ref, one_ref, two_ref, chip_ref, near_ref, far_ref, out_ref, staged, sent):
    total = chip_ref[3:4, :] + near_ref[3:4, :] + far_ref[4:5, :]
    step = 256
    copies = []
    for i in range(ROWS // step):
        here = slice(i * step, (i + 1) * step)
        one = jnp.where(within(2), one_ref[:, here], 0.0)
        two = jnp.where(within(-2), two_ref[:, here], 0.0)
        staged[here, :] = ((own_ref[:, here] + one + two) / total[:, here]).T
        copies.append(pltpu.make_async_copy(staged.at[here, :], out_ref.at[here, :], sent.at[i]))
        copies[-1].start()
    for copy in copies:
        copy.wait()


def exchanged(part):
    other = partner(part)
    chip = local(chip_body, plain((8, ROWS)), (part, other), name="chip_sum")
    one, two, three = toward(chip, 1), toward(chip, 2), toward(chip, 3)
    near = local(upper_body, plain((8, ROWS)), (one, two, three), name="near_sum")
    return (chip, near, partner(near)), (chip, three)


def shards(emb_a, emb_b, cat_a, cat_b, mass_a, mass_b, pair_list, pair_count):
    staged = [
        pltpu.VMEM((ROWS, WIDTH), F32),
        pltpu.VMEM((1, ROWS), jnp.int32),
        pltpu.VMEM((1, ROWS), F32),
        pltpu.SemaphoreType.DMA((3,)),
    ]
    slab = local(
        slab_body,
        plain((SLAB, ROWS)),
        tuple(map(outside, (emb_b, cat_b[None], mass_b[None]))),
        staged,
        far=3,
        name="slab",
    )
    ahead_one = toward(slab, 1)
    behind_one = away(slab, 1)
    other = partner(slab)
    left, wide_mass, on = local(
        left_body,
        (inside((ROWS, 4 * WIDTH), BF16), inside((ROWS, WIDTH)), FLAGS((8,), jnp.int32)),
        (pair_list, pair_count, *map(outside, (emb_a, cat_a[None], mass_a[None]))),
        staged,
        scalars=2,
        far=3,
        after=(slab,),
        name="left",
    )
    on = flagged(on)

    state, masses = (), [None] * SLOTS
    shapes = (inside((SLOTS, ROWS, ROWS)), inside((ROWS, WIDTH)), plain((8, ROWS)))

    def kernel_block(slot, slab):
        nonlocal state
        outs = shapes + ((plain((SLAB, ROWS)),) if slot in RELAYED else ())
        *state, masses[slot] = local(
            partial(block_body, slot),
            outs,
            (on, held(left), slab, *map(held, state)),
            [pltpu.VMEM((4 * WIDTH, ROWS), BF16)],
            scalars=1,
            us=2,
            aliases={3: 0, 4: 1} if state else None,
            name="kernel_block",
        )
        relayed = masses[slot]
        if slot in RELAYED:
            masses[slot] = state.pop()
        return relayed

    kernel_block(0, slab)
    kernel_block(1, other)
    third = beside(ahead_one)
    shared_two = partner(behind_one)
    shared = partner(ahead_one)
    kernel_block(3, behind_one)
    kernel_block(2, ahead_one)
    kernel_block(6, shared_two)
    kernel_block(5, shared)
    kernel_block(4, third)
    slabs = (slab, other, ahead_one, behind_one, third, shared, shared_two)
    kernels, sums = state
    kernels, part = local(
        first_body,
        (shapes[0], plain((8, ROWS))),
        (on, held(kernels), held(sums), held(wide_mass)),
        [pltpu.VMEM((ROWS, WIDTH), F32)],
        scalars=1,
        us=3,
        aliases={1: 0},
        name="first_scales",
    )
    totals, _ = exchanged(part)
    kernels, row_scale, part = local(
        second_body,
        (shapes[0], inside((ROWS, WIDTH)), plain((8, ROWS))),
        (on, held(kernels), *totals, *masses, held(wide_mass)),
        scalars=1,
        us=5,
        aliases={1: 0},
        name="second_scales",
    )
    totals, steps = exchanged(part)
    scaled = local(
        scaled_body,
        inside((2 * WIDTH, ROWS), BF16),
        (held(row_scale), emb_a),
        after=steps[:1],
        name="scaled_a",
    )

    def back_map(offset, *terms, after=()):
        nonlocal kernels
        kernels, out = local(
            partial(back_body, SLOT[offset]),
            (shapes[0], plain((WIDTH, ROWS))),
            (on, held(kernels), held(scaled), *terms),
            scalars=1,
            us=2,
            aliases={1: 0},
            after=after,
            name="back_map",
        )
        return out

    third = beside(back_map(-3))
    behind = partner(back_map(3))
    ahead = partner(back_map(-1, after=totals[1:2]))
    one = toward(back_map(-2, behind), 1)
    home = partner(back_map(1))
    two = away(back_map(2, ahead, third), 1)
    staged_out = [pltpu.VMEM((ROWS, WIDTH), F32), pltpu.SemaphoreType.DMA((4,))]
    state = ()
    for slot in range(SLOTS):
        last = slot == SLOTS - 1
        kernels, *state = local(
            partial(ahead_body, slot),
            (shapes[0], plain((ROWS, WIDTH))) if last else (shapes[0], shapes[1], shapes[1]),
            (on, held(kernels), slabs[slot], *totals, masses[slot], *map(held, state)),
            [pltpu.VMEM((2 * WIDTH, ROWS), BF16)] + (staged_out if last else []),
            scalars=1,
            us=2,
            aliases={1: 0, 7: 1, 8: 2} if state and not last else {1: 0},
            sent=(1,) if last else (),
            name="ahead_map",
        )
    mapped_a = state[0]
    own = back_map(0, home)
    mapped_b = local(
        last_body, plain((ROWS, WIDTH)), (own, one, two, *totals), staged_out, sent=(0,), name="last"
    )
    return (mapped_a, mapped_b)


def solution(mesh):
    placed = (
        P("dev", None),
        P("dev", None),
        P("dev"),
        P("dev"),
        P("dev"),
        P("dev"),
        P("dev", None),
        P("dev"),
    )
    return jax.shard_map(
        shards,
        mesh=mesh,
        in_specs=placed,
        out_specs=(P("dev", None), P("dev", None)),
        check_vma=False,
    )
```

```python
import math
from functools import partial

import jax
import jax.numpy as jnp
import ml_dtypes
import numpy as np
from jax import lax
from jax.experimental import pallas as pl
from jax.experimental.pallas import tpu as pltpu
from jax.sharding import PartitionSpec as P

ROWS = 1024
WIDTH = 128
SLAB = 136
CATS = 16
OFFSETS = (0, 1, 2, -2, -3, -1, 3)
SLOT = {offset: slot for slot, offset in enumerate(OFFSETS)}
SLOTS = 7
RELAYED = ()
SCALE = 10.0 * math.log2(math.e)
F32 = jnp.float32
BF16 = jnp.bfloat16
VMEM = pl.BlockSpec(memory_space=pltpu.VMEM)
SMEM = pl.BlockSpec(memory_space=pltpu.SMEM)
ANY = pl.BlockSpec(memory_space=pl.ANY)
MIB = 1024 * 1024


def three_parts(value):
    parts = []
    for _ in range(3):
        part = float(np.float32(value).astype(ml_dtypes.bfloat16))
        parts.append(part)
        value = value - part
    return parts


MATCH = three_parts(0.5 * SCALE)
BASE = three_parts(-1.5 * SCALE)


def held(array):
    return pltpu.with_memory_space_constraint(array, pltpu.VMEM)


def outside(array):
    return pltpu.with_memory_space_constraint(array, pltpu.HBM)


def inside(shape, dtype=F32):
    return pltpu.VMEM(shape, dtype)


def FLAGS(shape, dtype):
    return pltpu.SMEM(shape, dtype)


def flagged(array):
    return pltpu.with_memory_space_constraint(array, pltpu.SMEM)


def plain(shape, dtype=F32):
    return jax.ShapeDtypeStruct(shape, dtype)


def local(body, outs, operands, scratch=(), scalars=0, far=0, us=1, aliases=None, after=(), sent=(), name=None):
    near = len(operands) - scalars - far
    used = len(operands)

    def with_tokens(*refs):
        body(*refs[:used], *refs[used + len(after) :])

    several = outs if isinstance(outs, tuple) else (outs,)
    spaces = [SMEM if getattr(out, "memory_space", None) is pltpu.SMEM else VMEM for out in several]
    for index in sent:
        spaces[index] = ANY
    return pl.pallas_call(
        with_tokens,
        out_shape=outs,
        in_specs=[SMEM] * scalars + [VMEM] * near + [ANY] * (far + len(after)),
        out_specs=tuple(spaces) if isinstance(outs, tuple) else spaces[0],
        scratch_shapes=list(scratch),
        input_output_aliases=aliases or {},
        compiler_params=pltpu.CompilerParams(vmem_limit_bytes=4 * MIB),
        cost_estimate=pl.CostEstimate(
            flops=int(us * 1e9), transcendentals=0, bytes_accessed=int(us * 3e6)
        ),
        name=name,
    )(*operands, *after)


def partner(block):
    devices = lax.axis_size("dev")
    return lax.ppermute(block, "dev", [(i, i + 1 - 2 * (i % 2)) for i in range(devices)])


def beside(block):
    devices = lax.axis_size("dev")
    route = [(i, (i - 1 + 2 * (i % 2)) % devices) for i in range(devices)]
    return lax.ppermute(block, "dev", route)


def relayed(block, chips, way):
    devices = lax.axis_size("dev")
    route = []
    for i in range(devices):
        target = i + 2 * chips * way * (1 - 2 * (i % 2))
        if target < 0:
            target = -1 - target
        if target >= devices:
            target = 2 * devices - 1 - target
        route.append((i, target))
    return lax.ppermute(block, "dev", route)


def toward(block, chips):
    return relayed(block, chips, -1)


def away(block, chips):
    return relayed(block, chips, 1)


def within(offset):
    position = lax.axis_index("dev")
    there = position + offset * (1 - 2 * (position % 2))
    return (there >= 0) & (there < lax.axis_size("dev"))


def halves(x):
    high = x.astype(BF16)
    return high, (x - high.astype(F32)).astype(BF16)


def lanes_summed(x):
    total = x[:, 0:WIDTH]
    for j in range(1, x.shape[1] // WIDTH):
        total = total + x[:, j * WIDTH : (j + 1) * WIDTH]
    return total


def fetch_all(copies, arrived):
    started = []
    for index, (source, target) in enumerate(copies):
        copy = pltpu.make_async_copy(source, target, arrived.at[index])
        copy.start()
        started.append(copy)
    for copy in started:
        copy.wait()


def slab_body(b_ref, cat_ref, mass_ref, slab_ref, b, cat, mass, arrived):
    fetch_all(((b_ref, b), (cat_ref, cat), (mass_ref, mass)), arrived)
    slab_ref[0:WIDTH, :] = b[...].T
    pad = jnp.zeros((SLAB - WIDTH - 2, ROWS), F32)
    slab_ref[WIDTH:SLAB, :] = jnp.concatenate([cat[...].astype(F32), mass[...], pad], axis=0)


def left_body(list_ref, count_ref, a_ref, cat_ref, mass_ref, *refs):
    left_ref, wide_mass_ref, on_ref, a, cat, mass, arrived = refs
    fetch_all(((a_ref, a), (cat_ref, cat), (mass_ref, mass)), arrived)
    position = lax.axis_index("dev")
    sign = 1 - 2 * (position % 2)
    for slot, offset in enumerate(OFFSETS):
        on = jnp.int32(0)
        for entry in range(SLOTS):
            here = (list_ref[0, entry] == position + sign * offset) & (entry < count_ref[0])
            on = jnp.where(here, jnp.int32(1), on)
        on_ref[slot] = on
    unit = a[...] * lax.rsqrt(jnp.sum(a[...] * a[...], axis=1, keepdims=True) + 1e-06) * SCALE
    high, low = halves(unit)
    lane = lax.broadcasted_iota(jnp.int32, (ROWS, WIDTH), 1)
    wide_cat = jnp.broadcast_to(cat[...].astype(F32), (WIDTH, ROWS)).T
    same = (lane % CATS).astype(F32) == wide_cat
    match = jnp.where(lane < CATS, MATCH[0], jnp.where(lane < 2 * CATS, MATCH[1], MATCH[2]))
    base = jnp.where(lane == 3 * CATS, BASE[0], jnp.where(lane == 3 * CATS + 1, BASE[1], BASE[2]))
    bias = jnp.where(
        lane < 3 * CATS, jnp.where(same, match, 0.0), jnp.where(lane < 3 * CATS + 3, base, 0.0)
    )
    left_ref[:, 0:128] = high
    left_ref[:, 128:256] = low
    left_ref[:, 256:384] = high
    left_ref[:, 384:512] = bias.astype(BF16)
    wide_mass_ref[...] = jnp.broadcast_to(mass[...], (WIDTH, ROWS)).T


def block_body(slot, on_ref, left_ref, slab_ref, *refs):
    kernel_ref, sum_ref, mass_ref = refs[-4 - (slot in RELAYED) :][:3]
    right = refs[-1]
    mass_ref[...] = slab_ref[WIDTH:SLAB, :]
    if slot in RELAYED:
        refs[-2][...] = slab_ref[...]

    @pl.when(on_ref[slot] > 0)
    def _():
        v = slab_ref[0:WIDTH, :]
        v = v * lax.rsqrt(jnp.sum(v * v, axis=0, keepdims=True) + 1e-06)
        high, low = halves(v)
        row = lax.broadcasted_iota(jnp.int32, (WIDTH, ROWS), 0)
        same = (row % CATS).astype(F32) == slab_ref[WIDTH : WIDTH + 1, :]
        bias = jnp.where(row < 3 * CATS, same.astype(F32), (row < 3 * CATS + 3).astype(F32))
        right[0:128, :] = high
        right[128:256, :] = high
        right[256:384, :] = low
        right[384:512, :] = bias.astype(BF16)
        step = 256
        for i in range(ROWS // step):
            rows = slice(i * step, (i + 1) * step)
            kernel = jnp.exp2(jnp.dot(left_ref[rows, :], right[...], preferred_element_type=F32))
            kernel_ref[slot, rows, :] = kernel
            total = lanes_summed(kernel)
            sum_ref[rows, :] = total if slot == 0 else sum_ref[rows, :] + total


def column_parts(on_ref, kernels, scale_ref, part_ref):
    step = 32
    part_ref[...] = jnp.zeros((8, ROWS), F32)
    for slot, offset in enumerate(OFFSETS):

        def add(i, total, slot=slot):
            rows = pl.ds(pl.multiple_of(i * step, step), step)
            scale = scale_ref[rows, :]
            product = kernels[slot, rows, :] * jnp.concatenate([scale] * 8, axis=1)
            for t in range(step // 8):
                total = total + product[t * 8 : (t + 1) * 8]
            return total

        @pl.when(on_ref[slot] > 0)
        def _(add=add, offset=offset):
            total = lax.fori_loop(0, ROWS // step, add, jnp.zeros((8, ROWS), F32), unroll=8)
            part_ref[3 + offset : 4 + offset, :] = jnp.sum(total, axis=0, keepdims=True)


def first_body(on_ref, kernels, sum_ref, mass_ref, kernels_out, part_ref, scale):
    scale[...] = mass_ref[...] / jnp.sum(sum_ref[...], axis=1, keepdims=True)
    column_parts(on_ref, kernels, scale, part_ref)


def mirrored(x):
    return jnp.concatenate([x[7 - m : 8 - m] for m in range(8)], axis=0)


def chip_body(part_ref, other_ref, out_ref):
    out_ref[...] = part_ref[...] + mirrored(other_ref[...])


def upper_body(one_ref, two_ref, three_ref, out_ref):
    out = jnp.zeros((8, ROWS), F32)
    for chips, ref in ((1, one_ref), (2, two_ref), (3, three_ref)):
        rows = jnp.where(within(2 * chips), ref[0 : 8 - 2 * chips, :], 0.0)
        out = out + jnp.concatenate([jnp.zeros((2 * chips, ROWS), F32), rows], axis=0)
    out_ref[...] = out


def column_scales(totals, masses):
    chip_ref, near_ref, far_ref = totals
    total = chip_ref[...] + near_ref[...] + mirrored(far_ref[...])
    scales = []
    for slot, offset in enumerate(OFFSETS):
        here = total[3 + offset : 4 + offset]
        known = here > 0.0
        scales.append(jnp.where(known, masses[slot][1:2, :] / jnp.where(known, here, 1.0), 0.0))
    return scales


def second_body(on_ref, kernels, *refs):
    totals, masses = refs[0:3], refs[3:10]
    mass_ref, kernels_out, scale_ref, part_ref = refs[10:]
    step = 32
    for slot, scale in enumerate(column_scales(totals, masses)):

        def add(i, carry, slot=slot, wide=jnp.broadcast_to(scale, (8, ROWS))):
            for t in range(0, step, 8):
                rows = pl.ds(pl.multiple_of(i * step + t, 8), 8)
                total = lanes_summed(kernels[slot, rows, :] * wide)
                scale_ref[rows, :] = total if slot == 0 else scale_ref[rows, :] + total
            return carry

        @pl.when(on_ref[slot] > 0)
        def _(add=add):
            lax.fori_loop(0, ROWS // step, add, 0, unroll=8)

    scale_ref[...] = mass_ref[...] / jnp.sum(scale_ref[...], axis=1, keepdims=True)
    column_parts(on_ref, kernels, scale_ref, part_ref)


def scaled_body(scale_ref, a_ref, out_ref):
    high, low = halves((scale_ref[...] * a_ref[...]).T)
    out_ref[0:128, :] = high
    out_ref[128:256, :] = low


def back_body(slot, on_ref, kernels, scaled_ref, *rest):
    terms, out_ref = rest[:-2], rest[-1]
    step = 256

    @pl.when(on_ref[slot] > 0)
    def _():
        for j in range(ROWS // step):
            columns = slice(j * step, (j + 1) * step)
            high, low = halves(kernels[slot, :, columns])
            wide = jnp.dot(scaled_ref[...], high, preferred_element_type=F32)
            out = jnp.dot(scaled_ref[0:128, :], low, preferred_element_type=F32)
            out = out + wide[0:128] + wide[128:256]
            for term in terms:
                out = out + term[:, columns]
            out_ref[:, columns] = out

    @pl.when(on_ref[slot] == 0)
    def _():
        out = jnp.zeros((WIDTH, ROWS), F32)
        for term in terms:
            out = out + term[...]
        out_ref[...] = out


def ahead_body(slot, on_ref, kernels, slab_ref, chip_ref, near_ref, far_ref, mass_ref, *refs):
    final = slot == SLOTS - 1
    if final:
        sums, weights, kernels_out, out_ref, right, staged, sent = refs
    else:
        sums, weights, right = refs[-3:]
    m = 3 + OFFSETS[slot]
    step = 256
    across = (((1,), (1,)), ((), ()))
    chunks = [slice(i * step, (i + 1) * step) for i in range(ROWS // step)]

    def send(i):
        return pltpu.make_async_copy(staged.at[chunks[i], :], out_ref.at[chunks[i], :], sent.at[i])

    @pl.when(on_ref[slot] > 0)
    def _():
        total = chip_ref[m : m + 1, :] + near_ref[m : m + 1, :] + far_ref[7 - m : 8 - m, :]
        scale = mass_ref[1:2, :] / total
        high, low = halves(slab_ref[0:WIDTH, :] * scale)
        right[0:128, :] = high
        right[128:256, :] = low
        for i, rows in enumerate(chunks):
            kernel = kernels[slot, rows, :]
            weight = lanes_summed(kernel * scale)
            high, low = halves(kernel)
            wide = lax.dot_general(high, right[...], across, preferred_element_type=F32)
            part = lax.dot_general(low, right[0:128, :], across, preferred_element_type=F32)
            part = part + wide[:, 0:128] + wide[:, 128:256]
            if slot > 0:
                part = part + sums[rows, :]
                weight = weight + weights[rows, :]
            if final:
                staged[rows, :] = part / jnp.sum(weight, axis=1, keepdims=True)
                send(i).start()
            else:
                sums[rows, :] = part
                weights[rows, :] = weight

    if final:

        @pl.when(on_ref[slot] == 0)
        def _():
            for i, rows in enumerate(chunks):
                staged[rows, :] = sums[rows, :] / jnp.sum(weights[rows, :], axis=1, keepdims=True)
                send(i).start()

        for i in range(len(chunks)):
            send(i).wait()


def last_body(own_ref, one_ref, two_ref, chip_ref, near_ref, far_ref, out_ref, staged, sent):
    total = chip_ref[3:4, :] + near_ref[3:4, :] + far_ref[4:5, :]
    step = 256
    copies = []
    for i in range(ROWS // step):
        here = slice(i * step, (i + 1) * step)
        one = jnp.where(within(2), one_ref[:, here], 0.0)
        two = jnp.where(within(-2), two_ref[:, here], 0.0)
        staged[here, :] = ((own_ref[:, here] + one + two) / total[:, here]).T
        copies.append(pltpu.make_async_copy(staged.at[here, :], out_ref.at[here, :], sent.at[i]))
        copies[-1].start()
    for copy in copies:
        copy.wait()


def exchanged(part):
    other = partner(part)
    chip = local(chip_body, plain((8, ROWS)), (part, other), name="chip_sum")
    one, two, three = toward(chip, 1), toward(chip, 2), toward(chip, 3)
    near = local(upper_body, plain((8, ROWS)), (one, two, three), name="near_sum")
    return (chip, near, partner(near)), (chip, three)


def shards(emb_a, emb_b, cat_a, cat_b, mass_a, mass_b, pair_list, pair_count):
    staged = [
        pltpu.VMEM((ROWS, WIDTH), F32),
        pltpu.VMEM((1, ROWS), jnp.int32),
        pltpu.VMEM((1, ROWS), F32),
        pltpu.SemaphoreType.DMA((3,)),
    ]
    slab = local(
        slab_body,
        plain((SLAB, ROWS)),
        tuple(map(outside, (emb_b, cat_b[None], mass_b[None]))),
        staged,
        far=3,
        name="slab",
    )
    ahead_one = toward(slab, 1)
    behind_one = away(slab, 1)
    other = partner(slab)
    left, wide_mass, on = local(
        left_body,
        (inside((ROWS, 4 * WIDTH), BF16), inside((ROWS, WIDTH)), FLAGS((8,), jnp.int32)),
        (pair_list, pair_count, *map(outside, (emb_a, cat_a[None], mass_a[None]))),
        staged,
        scalars=2,
        far=3,
        after=(slab,),
        name="left",
    )
    on = flagged(on)

    state, masses = (), [None] * SLOTS
    shapes = (inside((SLOTS, ROWS, ROWS)), inside((ROWS, WIDTH)), plain((8, ROWS)))

    def kernel_block(slot, slab):
        nonlocal state
        outs = shapes + ((plain((SLAB, ROWS)),) if slot in RELAYED else ())
        *state, masses[slot] = local(
            partial(block_body, slot),
            outs,
            (on, held(left), slab, *map(held, state)),
            [pltpu.VMEM((4 * WIDTH, ROWS), BF16)],
            scalars=1,
            us=2,
            aliases={3: 0, 4: 1} if state else None,
            name="kernel_block",
        )
        relayed = masses[slot]
        if slot in RELAYED:
            masses[slot] = state.pop()
        return relayed

    kernel_block(0, slab)
    kernel_block(1, other)
    third = beside(ahead_one)
    shared_two = partner(behind_one)
    shared = partner(ahead_one)
    kernel_block(3, behind_one)
    kernel_block(2, ahead_one)
    kernel_block(6, shared_two)
    kernel_block(5, shared)
    kernel_block(4, third)
    slabs = (slab, other, ahead_one, behind_one, third, shared, shared_two)
    kernels, sums = state
    kernels, part = local(
        first_body,
        (shapes[0], plain((8, ROWS))),
        (on, held(kernels), held(sums), held(wide_mass)),
        [pltpu.VMEM((ROWS, WIDTH), F32)],
        scalars=1,
        us=3,
        aliases={1: 0},
        name="first_scales",
    )
    totals, _ = exchanged(part)
    kernels, row_scale, part = local(
        second_body,
        (shapes[0], inside((ROWS, WIDTH)), plain((8, ROWS))),
        (on, held(kernels), *totals, *masses, held(wide_mass)),
        scalars=1,
        us=5,
        aliases={1: 0},
        name="second_scales",
    )
    totals, steps = exchanged(part)
    scaled = local(
        scaled_body,
        inside((2 * WIDTH, ROWS), BF16),
        (held(row_scale), emb_a),
        after=steps[:1],
        name="scaled_a",
    )

    def back_map(offset, *terms, after=()):
        nonlocal kernels
        kernels, out = local(
            partial(back_body, SLOT[offset]),
            (shapes[0], plain((WIDTH, ROWS))),
            (on, held(kernels), held(scaled), *terms),
            scalars=1,
            us=2,
            aliases={1: 0},
            after=after,
            name="back_map",
        )
        return out

    third = beside(back_map(-3))
    behind = partner(back_map(3))
    ahead = partner(back_map(-1, after=totals[1:2]))
    one = toward(back_map(-2, behind), 1)
    two = away(back_map(2, ahead, third), 1)
    home = partner(back_map(1))
    staged_out = [pltpu.VMEM((ROWS, WIDTH), F32), pltpu.SemaphoreType.DMA((4,))]
    state = ()
    for slot in range(SLOTS):
        last = slot == SLOTS - 1
        kernels, *state = local(
            partial(ahead_body, slot),
            (shapes[0], plain((ROWS, WIDTH))) if last else (shapes[0], shapes[1], shapes[1]),
            (on, held(kernels), slabs[slot], *totals, masses[slot], *map(held, state)),
            [pltpu.VMEM((2 * WIDTH, ROWS), BF16)] + (staged_out if last else []),
            scalars=1,
            us=2,
            aliases={1: 0, 7: 1, 8: 2} if state and not last else {1: 0},
            sent=(1,) if last else (),
            name="ahead_map",
        )
    mapped_a = state[0]
    own = back_map(0, home)
    mapped_b = local(
        last_body, plain((ROWS, WIDTH)), (own, one, two, *totals), staged_out, sent=(0,), name="last"
    )
    return (mapped_a, mapped_b)


def solution(mesh):
    placed = (
        P("dev", None),
        P("dev", None),
        P("dev"),
        P("dev"),
        P("dev"),
        P("dev"),
        P("dev", None),
        P("dev"),
    )
    return jax.shard_map(
        shards,
        mesh=mesh,
        in_specs=placed,
        out_specs=(P("dev", None), P("dev", None)),
        check_vma=False,
    )
```
